256 devices in a mesh: seq: 64 (over z, x, core), chan: 4 (over y).
Axes of the slice: x: 4, y: 4, z: 8, core: 2. Of those that a mesh axis runs over, the one named last changes fastest.
Arguments:
- inputs: bfloat16 [8192, 2048], P('seq', 'chan'), may hold values from -6 to 6
- gate_branch: bfloat16 [8192, 2048], P('seq', 'chan'), may hold values from -6 to 6
- short_taps: float32 [4, 2048], P(None, 'chan'), may hold values from -3 to 3
- filters: float32 [8192, 2048], P('seq', 'chan'), may hold values from -0.0625 to 0.0625
- w_out: bfloat16 [2048, 2048], P('chan'), may hold values from -0.125 to 0.125
- cotangent: bfloat16 [8192, 2048], P('seq', 'chan'), may hold values from -16 to 16
Outputs:
- output: bfloat16 [8192, 2048], P('seq', 'chan')
- grad_inputs: bfloat16 [8192, 2048], P('seq', 'chan')
- grad_gate: bfloat16 [8192, 2048], P('seq', 'chan')
- grad_filters: float32 [8192, 2048], P('seq', 'chan')
- grad_taps: float32 [4, 2048], P(None, 'chan')
- grad_wout: float32 [2048, 2048], P('chan', 'seq')
The draws below stay inside these ranges and needn't reach their ends.
All inputs are finite; a program needn't handle non-finite values.
Results may differ from the reference program's by a relative error of at most 0.0047.
The reference program's roundings to bfloat16 on the way (of `gated`) count: a program that leaves them out, or rounds other values in their place, can miss the bound.
Values may be sent and summed in bfloat16 or wider, within the bound.
No kernel may reach another device: no remote copies, remote signals or barrier semaphores. Data moves between devices by JAX's collectives and lax.ppermute only.
A program may use at most 64 MiB of HBM per device.

```python
import jax
import jax.numpy as jnp

D = 2048
KS = 4
TOKENS = 8192


def raised(entries, key, source, target, parts, factor):
    owner, partner = [(jnp.arange(entries.shape[dim]) // (entries.shape[dim] // parts)).reshape([-1 if axis == dim else 1 for axis in range(entries.ndim)]) for dim in (source, target)]
    chosen = jax.random.permutation(key, parts)[partner]
    strong = (owner == chosen) | (owner == (partner + parts // 2) % parts)
    return jnp.where(strong, factor * entries, entries)


def block_levels(rng, shape, cuts, smallest, largest):
    loudness = 1.0
    for position, blocks in cuts:
        heights = jax.random.uniform(jax.random.fold_in(jax.random.fold_in(rng, 6), position), (blocks,), jnp.float32, smallest / len(cuts), largest / len(cuts))
        loudness = loudness * jnp.repeat(jnp.exp(heights), shape[position] // blocks).reshape((-1,) + (1,) * (len(shape) - 1 - position))
    return loudness


def normal_values(own_key, extent, deviation, most, split=(), kind=jnp.bfloat16):
    loudness = block_levels(own_key, extent, split, -0.22, 0.18) if split else 1.0
    values = jax.random.normal(own_key, extent, jnp.float32) * deviation * loudness
    return jnp.minimum(jnp.maximum(values, -most), most).astype(kind)


def bell_draw_with(own_key, extent, width, bound, shards, heavy, dtype=jnp.bfloat16):
    array = width * jax.random.normal(own_key, extent, jnp.float32)
    if shards:
        array = array * block_levels(own_key, extent, shards, -0.22, 0.18)
    return jnp.clip(raised(array, jax.random.fold_in(own_key, 3), *heavy), -bound, bound).astype(dtype)


def setup_inputs(seed: int = 0) -> dict:
    splits = jax.random.split(jax.random.key(seed), 7)
    inputs = normal_values(splits[0], (TOKENS, D), 1.0, 6.0, ((0, 64), (1, 4)))
    gate_branch = normal_values(splits[1], (TOKENS, D), 1.0, 6.0, ((0, 64), (1, 4)))
    short_taps = normal_values(splits[2], (KS, D), 0.5, 3.0, ((1, 4),), jnp.float32)
    filters = normal_values(splits[3], (TOKENS, D), TOKENS ** -0.5, 0.0625, ((0, 64), (1, 4)), jnp.float32)
    w_out = normal_values(splits[4], (D, D), D ** -0.5, 0.125, ((0, 4),))
    cotangent = bell_draw_with(splits[5], (TOKENS, D), 1.0, 16.0, ((0, 64), (1, 4)), (0, 1, 64, 4.0))
    return dict(inputs=inputs, gate_branch=gate_branch, short_taps=short_taps, filters=filters, w_out=w_out, cotangent=cotangent)


def spectrum(signal):
    padded = jnp.concatenate([signal, jnp.zeros_like(signal)], 0)
    return jnp.fft.rfft(padded, axis=0)


def back_transform(values):
    return jnp.fft.irfft(values, n=2 * TOKENS, axis=0)[:TOKENS].astype(jnp.float32)


def reference(inputs, gate_branch, short_taps, filters, w_out, cotangent):
    widened = inputs.astype(jnp.float32)
    padded = jnp.pad(widened, ((KS - 1, 0), (0, 0)))
    mixed = jnp.zeros_like(widened)
    for tap_index in range(KS):
        mixed = mixed + short_taps[tap_index] * padded[KS - 1 - tap_index:KS - 1 - tap_index + TOKENS]
    mixed_spec = spectrum(mixed)
    filter_spec = spectrum(filters)
    convolved = back_transform(mixed_spec * filter_spec)
    gate_wide = gate_branch.astype(jnp.float32)
    gated = (gate_wide * convolved).astype(jnp.bfloat16)
    output = jnp.dot(gated, w_out, preferred_element_type=jnp.float32).astype(jnp.bfloat16)
    grad_gated = jnp.dot(cotangent, w_out.T, preferred_element_type=jnp.float32)
    grad_gate = (grad_gated * convolved).astype(jnp.bfloat16)
    grad_conv = grad_gated * gate_wide
    grad_spec = spectrum(grad_conv)
    grad_mixed = back_transform(jnp.conj(filter_spec) * grad_spec)
    grad_filters = back_transform(jnp.conj(mixed_spec) * grad_spec)
    grad_padded = jnp.pad(grad_mixed, ((0, KS - 1), (0, 0)))
    grad_wide = jnp.zeros_like(widened)
    tap_rows = []
    for tap_index in range(KS):
        grad_wide = grad_wide + short_taps[tap_index] * grad_padded[tap_index:tap_index + TOKENS]
        shifted = padded[KS - 1 - tap_index:KS - 1 - tap_index + TOKENS]
        tap_rows.append(jnp.sum(shifted * grad_mixed, axis=0))
    grad_inputs = grad_wide.astype(jnp.bfloat16)
    grad_taps = jnp.stack(tap_rows, 0)
    grad_wout = jnp.dot(gated.T, cotangent, preferred_element_type=jnp.float32)
    return output, grad_inputs, grad_gate, grad_filters, grad_taps, grad_wout
```

```python
import functools
import math

import jax
import jax.numpy as jnp
import ml_dtypes
import numpy as np
from jax import lax
from jax.experimental import pallas as pl
from jax.experimental.pallas import tpu as pltpu
from jax.sharding import PartitionSpec as P

F32 = jnp.float32
BF16 = jnp.bfloat16
VMEM = pl.BlockSpec(memory_space=pltpu.VMEM)
SMEM = pl.BlockSpec(memory_space=pltpu.SMEM)


def split_table(table):
    high = table.astype(ml_dtypes.bfloat16)
    low = (table - high.astype(np.float64)).astype(ml_dtypes.bfloat16)
    return high, low


def transform_tables(coarse, fine):
    length = coarse * fine
    k1 = np.arange(coarse)[:, None] + 0.25
    angle = 2.0 * math.pi * k1 * np.arange(coarse)[None, :] / coarse
    first = np.concatenate([np.cos(angle), -np.sin(angle)], 0)
    high, low = split_table(first)
    first_cat = np.concatenate([high, high, low], 1)
    last = np.concatenate([np.cos(angle).T, -np.sin(angle).T], 1)
    high, low = split_table(last)
    last_cat = np.concatenate([high, high, low], 1)
    angle = 2.0 * math.pi * k1 * np.arange(fine)[None, :] / length
    twist = np.stack([np.cos(angle), np.sin(angle)], 0).astype(np.float32)
    angle = 2.0 * math.pi * (np.outer(np.arange(fine), np.arange(fine)) % fine) / fine
    cos, sin = np.cos(angle), np.sin(angle)
    forward = np.concatenate([np.concatenate([cos, -sin], 1), np.concatenate([sin, cos], 1)], 0)
    inverse = np.concatenate([np.concatenate([cos, sin], 1), np.concatenate([-sin, cos], 1)], 0) / length
    second = np.stack([*split_table(forward), *split_table(inverse)], 0)
    return first_cat, last_cat, twist, second


def split(value):
    high = value.astype(BF16)
    return high, (value - high.astype(F32)).astype(BF16)


def dot(a, b, dims=(((1,), (0,)), ((), ()))):
    return lax.dot_general(a, b, dims, preferred_element_type=F32)


NT = (((1,), (1,)), ((), ()))


def pre_kernel(me_ref, inputs_ref, filters_ref, gate_ref, w_ref, c0, c1, c2, c3, out_ref, gg_ref):
    chan = me_ref[1]
    width = inputs_ref.shape[1]
    owners = out_ref.shape[0]
    total = None
    for step, piece in enumerate((c0, c1, c2, c3)):
        owner = lax.rem(chan + 4 - step, 4)
        cols = pl.ds(pl.multiple_of(owner * width, width), width)
        term = dot(w_ref[:, cols], piece[...], NT)
        total = term if total is None else total + term
    gg_ref[...] = total
    grad_conv = total * gate_ref[...].astype(F32).T
    rows = [inputs_ref[...].astype(F32).T]
    filters = filters_ref[...].T
    high = filters.astype(BF16).astype(F32)
    rows += [high, grad_conv, filters - high]
    rows = [r.reshape(owners, 8, r.shape[1]) for r in rows]
    out_ref[...] = jnp.concatenate(rows, 1).astype(BF16)


def cot_kernel(me_ref, c0, c1, c2, c3, own_ref, send_ref, scratch):
    core = lax.rem(me_ref[0], 2)
    chan = me_ref[1]
    for step, piece in enumerate((c0, c1, c2, c3)):
        owner = lax.rem(chan + 4 - step, 4)
        flipped = piece[...].astype(F32).T.astype(BF16)
        scratch[pl.ds(owner * 8, 8)] = flipped.reshape(8, 2, 32, flipped.shape[1])
    own_ref[...] = scratch[:, core]
    send_ref[...] = scratch[:, 1 - core]


def conv_kernel(taps_ref, recv_ref, first_ref, last_ref, twist_ref, second_ref, out_ref, sig, stage, spec):
    blocks, _, fine = recv_ref.shape
    taps = taps_ref[...]
    lane = lax.broadcasted_iota(jnp.int32, (blocks, 8, fine), 2)
    received = recv_ref[...].astype(F32)
    given = received[:, 0:8]
    zero = jnp.zeros((1, 8, fine), F32)

    def delayed(value, t):
        if t == 0:
            return value
        turned = pltpu.roll(value, t, 2)
        return jnp.where(lane < t, jnp.concatenate([zero, turned[:-1]], 0), turned)

    mixed = jnp.zeros_like(given)
    for t in range(4):
        mixed = mixed + taps[:, t : t + 1][None] * delayed(given, t)
    sig[0] = mixed.reshape(blocks * 8, fine)
    sig[1] = (received[:, 8:16] + received[:, 24:32]).reshape(blocks * 8, fine)
    sig[2] = received[:, 16:24].reshape(blocks * 8, fine)

    twist_re, twist_im = twist_ref[0], twist_ref[1]
    for s in range(3):
        for pair in range(4):
            both = jnp.concatenate([sig[s, pl.ds(2 * pair + h, blocks, stride=8), :] for h in range(2)], 1)
            high, low = split(both)
            coarse = dot(first_ref[...], jnp.concatenate([high, low, high], 0))
            for h in range(2):
                re = coarse[:blocks, h * fine : (h + 1) * fine]
                im = coarse[blocks:, h * fine : (h + 1) * fine]
                new_re = re * twist_re + im * twist_im
                new_im = im * twist_re - re * twist_im
                rows = pl.ds((s * 8 + 2 * pair + h) * blocks, blocks)
                high, low = split(jnp.concatenate([new_re, new_im], 1))
                stage[rows, : 2 * fine] = high
                stage[rows, 2 * fine :] = low

    def second(rows, which):
        high = stage[rows, : 2 * fine]
        low = stage[rows, 2 * fine :]
        return dot(high, second_ref[which]) + dot(low, second_ref[which]) + dot(high, second_ref[which + 1])

    count = 8 * blocks
    for s in range(3):
        spec[pl.ds(s * count, count), :] = second(pl.ds(s * count, count), 0)
    for c in range(8):
        parts = []
        for s in range(3):
            rows = pl.ds((s * 8 + c) * blocks, blocks)
            parts.append((spec[rows, :fine], spec[rows, fine:]))
        (mr, mi), (fr, fi), (gr, gi) = parts
        products = (
            (mr * fr - mi * fi, mr * fi + mi * fr),
            (fr * gr + fi * gi, fr * gi - fi * gr),
            (mr * gr + mi * gi, mr * gi - mi * gr),
        )
        for s in range(3):
            rows = pl.ds((s * 8 + c) * blocks, blocks)
            high, low = split(jnp.concatenate(products[s], 1))
            stage[rows, : 2 * fine] = high
            stage[rows, 2 * fine :] = low
    for s in range(3):
        spec[pl.ds(s * count, count), :] = second(pl.ds(s * count, count), 2)
    for s in range(3):
        for pair in range(4):
            halves = []
            for h in range(2):
                rows = pl.ds((s * 8 + 2 * pair + h) * blocks, blocks)
                re, im = spec[rows, :fine], spec[rows, fine:]
                halves.append(jnp.concatenate([re * twist_re - im * twist_im, im * twist_re + re * twist_im], 0))
            high, low = split(jnp.concatenate(halves, 1))
            back = dot(last_ref[...], jnp.concatenate([high, low, high], 0))
            for h in range(2):
                sig[s, pl.ds(2 * pair + h, blocks, stride=8), :] = back[:, h * fine : (h + 1) * fine]

    convolved, grad_mixed, grad_filters = (sig[s].reshape(blocks, 8, fine) for s in range(3))
    grad_inputs = taps[:, 0:1][None] * grad_mixed
    for t in range(1, 4):
        turned = pltpu.roll(grad_mixed, fine - t, 2)
        ahead = jnp.where(lane >= fine - t, jnp.concatenate([turned[1:], zero], 0), turned)
        grad_inputs = grad_inputs + taps[:, t : t + 1][None] * ahead
    column = lax.broadcasted_iota(jnp.int32, (8, fine), 1)
    tap_tile = jnp.zeros((8, fine), F32)
    for t in range(4):
        total = jnp.sum(jnp.sum(delayed(given, t) * grad_mixed, axis=0), axis=1, keepdims=True)
        high = total.astype(BF16).astype(F32)
        tap_tile = jnp.where(column == t, high, tap_tile)
        tap_tile = jnp.where(column == t + 4, total - high, tap_tile)
    tap_rows = jnp.broadcast_to(tap_tile[None], (blocks, 8, fine))
    out_ref[...] = jnp.concatenate([convolved, grad_inputs, grad_filters, tap_rows], 1).astype(BF16)


def gate_kernel(recv_ref, gate_ref, gated_ref):
    blocks, _, rows = recv_ref.shape
    convolved = recv_ref[:, 0:16].astype(F32)[:, 0:8].reshape(blocks * 8, rows)
    gated_ref[...] = (gate_ref[...].astype(F32) * convolved.T).astype(BF16)


def weight_kernel(cot_own, cot_other, gated_own, gated_other, out_ref):
    depth = cot_own.shape[2]
    left = cot_own[...].reshape(-1, depth)
    right = cot_other[...].reshape(-1, depth)
    total = dot(left, gated_own[...]) + dot(right, gated_other[...])
    out_ref[...] = total.reshape(out_ref.shape).astype(BF16)


def post_kernel(me_ref, recv_ref, gated_ref, gg_ref, w_ref, gi_ref, gate_grad_ref, gf_ref, taps_ref, own_ref, s1, s2, s3):
    chan = me_ref[1]
    blocks, _, rows = recv_ref.shape
    width = blocks * 8
    received = recv_ref[...].astype(F32)
    convolved = received[:, 0:8].reshape(width, rows)
    gate_grad_ref[...] = (gg_ref[...] * convolved).T.astype(BF16)
    gi_ref[...] = received[:, 8:16].reshape(width, rows).T.astype(BF16)
    gf_ref[...] = received[:, 16:24].reshape(width, rows).T
    flat = received[:, 24:32].reshape(width, rows).T
    taps_ref[...] = flat[0:4] + flat[4:8]
    for step, out in enumerate((own_ref, s1, s2, s3)):
        owner = lax.rem(chan + step, 4)
        cols = pl.ds(pl.multiple_of(owner * width, width), width)
        out[...] = dot(gated_ref[...], w_ref[:, cols]).astype(out.dtype)


def sum_kernel(recv_ref, out_ref):
    out_ref[...] = jnp.sum(recv_ref[...].astype(F32), axis=0).T


def call(kernel, outs, in_specs, scratch=()):
    return pl.pallas_call(
        kernel,
        out_shape=outs,
        in_specs=in_specs,
        out_specs=jax.tree.map(lambda _: VMEM, outs),
        scratch_shapes=list(scratch),
        compiler_params=pltpu.CompilerParams(vmem_limit_bytes=50 * 1024 * 1024),
    )


def shifted(value, axis, steps):
    count = lax.axis_size(axis)
    return lax.ppermute(value, axis, [(i, (i + steps) % count) for i in range(count)])


def local(inputs, gate_branch, short_taps, filters, w_out, cotangent):
    shape = jax.ShapeDtypeStruct
    owners = lax.axis_size("seq")
    rows, width = inputs.shape
    me = jnp.stack([lax.axis_index("seq"), lax.axis_index("chan")]).astype(jnp.int32)
    tables = transform_tables(owners, rows)
    my_taps = lax.dynamic_slice_in_dim(short_taps, me[0] * 8, 8, 1).T

    pieces = [cotangent] + [shifted(cotangent, "chan", d) for d in (1, 2, 3)]
    packed, grad_gated = call(
        pre_kernel,
        (shape((owners, 32, rows), BF16), shape((width, rows), F32)),
        [SMEM] + [VMEM] * 8,
    )(me, inputs, filters, gate_branch, w_out, *pieces)
    received = lax.all_to_all(packed, "seq", 0, 0, tiled=True)

    cot_own, cot_send = call(
        cot_kernel,
        (shape((32, 32, rows), BF16), shape((32, 32, rows), BF16)),
        [SMEM] + [VMEM] * 4,
        [pltpu.VMEM((32, 2, 32, rows), BF16)],
    )(me, *pieces)
    swap = [(i, i ^ 1) for i in range(owners)]
    cot_other = lax.ppermute(cot_send, "seq", swap)

    returned = call(
        conv_kernel,
        shape((owners, 32, rows), BF16),
        [VMEM] * 6,
        [
            pltpu.VMEM((3, width, rows), F32),
            pltpu.VMEM((3 * width, 4 * rows), BF16),
            pltpu.VMEM((3 * width, 2 * rows), F32),
        ],
    )(my_taps, received, *[jnp.asarray(t) for t in tables])
    arrived = lax.all_to_all(returned, "seq", 0, 0, tiled=True)

    gated = call(gate_kernel, shape((rows, width), BF16), [VMEM] * 2)(arrived, gate_branch)
    gated_other = lax.ppermute(gated, "seq", swap)
    weight_terms = call(weight_kernel, shape((32, 32, width), BF16), [VMEM] * 4)(
        cot_own, cot_other, gated, gated_other
    )
    groups = [list(range(k, owners, 2)) for k in range(2)]
    weight_parts = lax.all_to_all(weight_terms, "seq", 0, 0, axis_index_groups=groups, tiled=True)

    grad_inputs, grad_gate, grad_filters, grad_taps, own, s1, s2, s3 = call(
        post_kernel,
        (
            shape((rows, width), BF16),
            shape((rows, width), BF16),
            shape((rows, width), F32),
            shape((4, width), F32),
            shape((rows, width), F32),
        )
        + (shape((rows, width), BF16),) * 3,
        [SMEM] + [VMEM] * 4,
    )(me, arrived, gated, grad_gated, w_out)
    others = [shifted(s, "chan", d) for d, s in ((1, s1), (2, s2), (3, s3))]
    output = (own + others[0].astype(F32) + others[1].astype(F32) + others[2].astype(F32)).astype(BF16)

    grad_wout = call(sum_kernel, shape((width, 32), F32), [VMEM])(weight_parts)
    return (output, grad_inputs, grad_gate, grad_filters, grad_taps, grad_wout)


def solution(mesh):
    in_specs = (
        P("seq", "chan"),
        P("seq", "chan"),
        P(None, "chan"),
        P("seq", "chan"),
        P("chan", None),
        P("seq", "chan"),
    )
    out_specs = (
        P("seq", "chan"),
        P("seq", "chan"),
        P("seq", "chan"),
        P("seq", "chan"),
        P(None, "chan"),
        P("chan", "seq"),
    )
    return jax.shard_map(local, mesh=mesh, in_specs=in_specs, out_specs=out_specs, check_vma=False)
```

```python
import functools
import math

import jax
import jax.numpy as jnp
import ml_dtypes
import numpy as np
from jax import lax
from jax.experimental import pallas as pl
from jax.experimental.pallas import tpu as pltpu
from jax.sharding import PartitionSpec as P

F32 = jnp.float32
BF16 = jnp.bfloat16
VMEM = pl.BlockSpec(memory_space=pltpu.VMEM)
SMEM = pl.BlockSpec(memory_space=pltpu.SMEM)
ANY = pl.BlockSpec(memory_space=pl.ANY)


def split_table(table):
    high = table.astype(ml_dtypes.bfloat16)
    low = (table - high.astype(np.float64)).astype(ml_dtypes.bfloat16)
    return high, low


def transform_tables(coarse, fine):
    length = coarse * fine
    k1 = np.arange(coarse)[:, None] + 0.25
    angle = 2.0 * math.pi * k1 * np.arange(coarse)[None, :] / coarse
    first = np.concatenate([np.cos(angle), -np.sin(angle)], 0)
    high, low = split_table(first)
    first_cat = np.concatenate([high, high, low], 1)
    last = np.concatenate([np.cos(angle).T, -np.sin(angle).T], 1)
    high, low = split_table(last)
    last_cat = np.concatenate([high, high, low], 1)
    angle = 2.0 * math.pi * k1 * np.arange(fine)[None, :] / length
    twist = np.stack([np.cos(angle), np.sin(angle)], 0).astype(np.float32)
    angle = 2.0 * math.pi * (np.outer(np.arange(fine), np.arange(fine)) % fine) / fine
    cos, sin = np.cos(angle), np.sin(angle)
    forward = np.concatenate([np.concatenate([cos, -sin], 1), np.concatenate([sin, cos], 1)], 0)
    inverse = np.concatenate([np.concatenate([cos, sin], 1), np.concatenate([-sin, cos], 1)], 0) / length
    second = np.stack([*split_table(forward), *split_table(inverse)], 0)
    return first_cat, last_cat, twist, second


def split(value):
    high = value.astype(BF16)
    return high, (value - high.astype(F32)).astype(BF16)


def dot(a, b, dims=(((1,), (0,)), ((), ()))):
    return lax.dot_general(a, b, dims, preferred_element_type=F32)


NT = (((1,), (1,)), ((), ()))


def load(sources, buffers, sems):
    copies = [pltpu.make_async_copy(src, dst, sems.at[i]) for i, (src, dst) in enumerate(zip(sources, buffers))]
    for copy in copies:
        copy.start()
    for copy in copies:
        copy.wait()


def pack_kernel(inputs_hbm, filters_hbm, out_ref, inputs_ref, filters_ref, sems):
    load((inputs_hbm, filters_hbm), (inputs_ref, filters_ref), sems)
    owners = out_ref.shape[0]
    filters = filters_ref[...].T
    high = filters.astype(BF16).astype(F32)
    rows = [inputs_ref[...].astype(F32).T, high, filters - high]
    rows = [r.reshape(owners, 8, r.shape[1]) for r in rows]
    out_ref[...] = jnp.concatenate(rows, 1).astype(BF16)


def cotangent_kernel(me_ref, gate_hbm, w_hbm, c0_hbm, c1, c2, c3, out_ref, gg_ref, gate_ref, w_ref, c0, sems):
    load((gate_hbm, w_hbm, c0_hbm), (gate_ref, w_ref, c0), sems)
    chan = me_ref[1]
    width = gate_ref.shape[1]
    total = None
    for step, piece in enumerate((c0, c1, c2, c3)):
        owner = lax.rem(chan + 4 - step, 4)
        cols = pl.ds(pl.multiple_of(owner * width, width), width)
        term = dot(w_ref[:, cols], piece[...], NT)
        total = term if total is None else total + term
    gg_ref[...] = total
    out_ref[...] = (total * gate_ref[...].astype(F32).T).astype(BF16)


def cot_kernel(me_ref, c0, c1, c2, c3, o0, o1, o2, o3, scratch):
    kind = lax.rem(me_ref[0], 4)
    chan = me_ref[1]
    for step, piece in enumerate((c0, c1, c2, c3)):
        owner = lax.rem(chan + 4 - step, 4)
        flipped = piece[...].astype(F32).T.astype(BF16)
        scratch[pl.ds(owner * 4, 4)] = flipped.reshape(4, 4, 32, flipped.shape[1])
    for d, out in enumerate((o0, o1, o2, o3)):
        out[...] = scratch[:, kind ^ d]


def delayed(value, t):
    if t == 0:
        return value
    lane = lax.broadcasted_iota(jnp.int32, value.shape, 2)
    turned = pltpu.roll(value, t, 2)
    before = jnp.concatenate([jnp.zeros_like(turned[:1]), turned[:-1]], 0)
    return jnp.where(lane < t, before, turned)


def coarse_stage(sig, s, first_ref, twist_ref, stage):
    blocks, fine = twist_ref.shape[1:]
    twist_re, twist_im = twist_ref[0], twist_ref[1]
    for pair in range(4):
        both = jnp.concatenate([sig[s, pl.ds(2 * pair + h, blocks, stride=8), :] for h in range(2)], 1)
        high, low = split(both)
        coarse = dot(first_ref[...], jnp.concatenate([high, low, high], 0))
        for h in range(2):
            re = coarse[:blocks, h * fine : (h + 1) * fine]
            im = coarse[blocks:, h * fine : (h + 1) * fine]
            put(stage, s, 2 * pair + h, re * twist_re + im * twist_im, im * twist_re - re * twist_im)


def put(stage, s, c, re, im):
    blocks, fine = re.shape
    rows = pl.ds((s * 8 + c) * blocks, blocks)
    high, low = split(jnp.concatenate([re, im], 1))
    stage[rows, : 2 * fine] = high
    stage[rows, 2 * fine :] = low


def fine_stage(stage, s, second_ref, which):
    count = stage.shape[1]
    rows = pl.ds(s * count, count)
    high = stage[rows, : stage.shape[1] // 2]
    low = stage[rows, stage.shape[1] // 2 :]
    return dot(high, second_ref[which]) + dot(low, second_ref[which]) + dot(high, second_ref[which + 1])


def back_stage(spec, s, last_ref, twist_ref, sig):
    blocks, fine = twist_ref.shape[1:]
    twist_re, twist_im = twist_ref[0], twist_ref[1]
    for pair in range(4):
        halves = []
        for h in range(2):
            rows = pl.ds((s * 8 + 2 * pair + h) * blocks, blocks)
            re, im = spec[rows, :fine], spec[rows, fine:]
            halves.append(jnp.concatenate([re * twist_re - im * twist_im, im * twist_re + re * twist_im], 0))
        high, low = split(jnp.concatenate(halves, 1))
        back = dot(last_ref[...], jnp.concatenate([high, low, high], 0))
        for h in range(2):
            sig[s, pl.ds(2 * pair + h, blocks, stride=8), :] = back[:, h * fine : (h + 1) * fine]


def forward_kernel(taps_ref, recv_ref, grad_ref, first_ref, last_ref, twist_ref, second_ref, out_ref, spec, sig, stage, work):
    blocks, _, fine = recv_ref.shape
    count = 8 * blocks
    taps = taps_ref[...]
    received = recv_ref[...].astype(F32)
    given = received[:, 0:8]
    mixed = jnp.zeros_like(given)
    for t in range(4):
        mixed = mixed + taps[:, t : t + 1][None] * delayed(given, t)
    sig[0] = mixed.reshape(count, fine)
    sig[1] = (received[:, 8:16] + received[:, 16:24]).reshape(count, fine)
    for s in range(2):
        coarse_stage(sig, s, first_ref, twist_ref, stage)
    for s in range(2):
        spec[pl.ds(s * count, count), :] = fine_stage(stage, s, second_ref, 0)
    for c in range(8):
        (mr, mi), (fr, fi) = (
            (spec[pl.ds((s * 8 + c) * blocks, blocks), :fine], spec[pl.ds((s * 8 + c) * blocks, blocks), fine:])
            for s in range(2)
        )
        put(stage, 0, c, mr * fr - mi * fi, mr * fi + mi * fr)
    work[...] = fine_stage(stage, 0, second_ref, 2)
    back_stage(work, 0, last_ref, twist_ref, sig)
    convolved = sig[0].reshape(blocks, 8, fine)
    grad_conv = grad_ref[...].astype(F32).reshape(blocks, 8, fine)
    out_ref[...] = jnp.concatenate([convolved, grad_conv], 1).astype(BF16)


def backward_kernel(
    me_ref, taps_ref, recv_ref, back_ref, spec, first_ref, last_ref, twist_ref, second_ref,
    o0, o1, o2, o3, sig, stage, work, parts
):
    blocks, _, fine = recv_ref.shape
    count = 8 * blocks
    taps = taps_ref[...]
    sig[0] = back_ref[...].astype(F32)[:, 8:16].reshape(count, fine)
    coarse_stage(sig, 0, first_ref, twist_ref, stage)
    work[pl.ds(0, count), :] = fine_stage(stage, 0, second_ref, 0)
    for c in range(8):
        rows = pl.ds(c * blocks, blocks)
        gr, gi = work[rows, :fine], work[rows, fine:]
        for s in range(2):
            rows = pl.ds(((1 - s) * 8 + c) * blocks, blocks)
            re, im = spec[rows, :fine], spec[rows, fine:]
            put(stage, s, c, re * gr + im * gi, re * gi - im * gr)
    for s in range(2):
        work[pl.ds(s * count, count), :] = fine_stage(stage, s, second_ref, 2)
    for s in range(2):
        back_stage(work, s, last_ref, twist_ref, sig)
    grad_mixed, grad_filters = (sig[s].reshape(blocks, 8, fine) for s in range(2))
    lane = lax.broadcasted_iota(jnp.int32, (blocks, 8, fine), 2)
    zero = jnp.zeros((1, 8, fine), F32)
    grad_inputs = taps[:, 0:1][None] * grad_mixed
    for t in range(1, 4):
        turned = pltpu.roll(grad_mixed, fine - t, 2)
        ahead = jnp.where(lane >= fine - t, jnp.concatenate([turned[1:], zero], 0), turned)
        grad_inputs = grad_inputs + taps[:, t : t + 1][None] * ahead
    given = recv_ref[...].astype(F32)[:, 0:8]
    column = lax.broadcasted_iota(jnp.int32, (8, fine), 1)
    tap_tile = jnp.zeros((8, fine), F32)
    for t in range(4):
        total = jnp.sum(jnp.sum(delayed(given, t) * grad_mixed, axis=0), axis=1, keepdims=True)
        high = total.astype(BF16).astype(F32)
        tap_tile = jnp.where(column == t, high, tap_tile)
        tap_tile = jnp.where(column == t + 4, total - high, tap_tile)
    tap_rows = jnp.broadcast_to(tap_tile[None], (blocks, 8, fine))
    parts[...] = jnp.concatenate([grad_inputs, grad_filters, tap_rows], 1).reshape(blocks // 4, 4, 24, fine)
    kind = lax.rem(me_ref[0], 4)
    for d, out in enumerate((o0, o1, o2, o3)):
        out[...] = parts[:, kind ^ d].astype(BF16)


def gate_kernel(recv_ref, gate_ref, gated_ref):
    blocks, _, rows = recv_ref.shape
    convolved = recv_ref[...].astype(F32)[:, 0:8].reshape(blocks * 8, rows)
    gated_ref[...] = (gate_ref[...].astype(F32) * convolved.T).astype(BF16)


def weight_kernel(k0, k1, k2, k3, g0, g1, g2, g3, p0, p1, p2, p3, out_ref):
    groups, rows, depth = k0.shape
    left = jnp.concatenate([k[...].reshape(groups * rows, depth) for k in (k0, k1, k2, k3)], 1)
    total = dot(left, jnp.concatenate([g[...] for g in (g0, g1, g2, g3)], 0))
    for j in range(4):
        columns = total[:, j * depth : (j + 1) * depth].reshape(groups, rows, depth)
        out_ref[:, 64 + j * rows : 64 + (j + 1) * rows, :] = columns.astype(BF16)
    tap_rows = None
    for d, part in enumerate((p0, p1, p2, p3)):
        value = part[...].astype(F32)
        out_ref[:, 16 * d : 16 * (d + 1), :] = value[:, 0:16].astype(BF16)
        tile = pltpu.roll(value[:, 16:24], 8 * d, 2) if d else value[:, 16:24]
        tap_rows = tile if tap_rows is None else tap_rows + tile
    out_ref[:, 192:208, :] = jnp.concatenate([tap_rows, jnp.zeros_like(tap_rows)], 1).astype(BF16)


def project_kernel(me_ref, recv_ref, gated_ref, gg_ref, w_ref, gate_grad_ref, own_ref, s1, s2, s3):
    chan = me_ref[1]
    blocks, _, rows = recv_ref.shape
    width = gated_ref.shape[1]
    convolved = recv_ref[...].astype(F32)[:, 0:8].reshape(width, rows)
    gate_grad_ref[...] = (gg_ref[...] * convolved).T.astype(BF16)
    for step, out in enumerate((own_ref, s1, s2, s3)):
        owner = lax.rem(chan + step, 4)
        cols = pl.ds(pl.multiple_of(owner * width, width), width)
        out[...] = dot(gated_ref[...], w_ref[:, cols]).astype(out.dtype)


def unpack_kernel(me_ref, recv_ref, gi_ref, gf_ref, taps_ref, weight_ref, scratch):
    kind = lax.rem(me_ref[0], 4)
    groups, _, rows = recv_ref.shape
    width = groups * 32
    tap_rows = recv_ref[:, 192:208, :].astype(F32)[:, 0:8]
    for d in range(4):
        value = recv_ref[:, 16 * d : 16 * (d + 1), :].astype(F32)
        source = kind ^ d
        scratch[0, :, source] = value[:, 0:8]
        scratch[1, :, source] = value[:, 8:16]
        scratch[2, :, source] = pltpu.roll(tap_rows, rows - 8 * d, 2) if d else tap_rows
    gi_ref[...] = scratch[0].reshape(width, rows).T.astype(BF16)
    gf_ref[...] = scratch[1].reshape(width, rows).T
    flat = scratch[2].reshape(width, rows).T
    taps_ref[...] = flat[0:4] + flat[4:8]
    total = jnp.sum(recv_ref[:, 64:192, :].astype(F32), axis=0)
    for j in range(4):
        weight_ref[:, j * rows : (j + 1) * rows] = total[32 * j : 32 * (j + 1)]


def call(kernel, outs, in_specs, scratch=()):
    return pl.pallas_call(
        kernel,
        out_shape=outs,
        in_specs=in_specs,
        out_specs=jax.tree.map(lambda _: VMEM, outs),
        scratch_shapes=list(scratch),
        compiler_params=pltpu.CompilerParams(vmem_limit_bytes=50 * 1024 * 1024),
    )


def shifted(value, axis, steps):
    count = lax.axis_size(axis)
    return lax.ppermute(value, axis, [(i, (i + steps) % count) for i in range(count)])


def local(inputs, gate_branch, short_taps, filters, w_out, cotangent):
    shape = jax.ShapeDtypeStruct
    owners = lax.axis_size("seq")
    rows, width = inputs.shape
    me = jnp.stack([lax.axis_index("seq"), lax.axis_index("chan")]).astype(jnp.int32)
    tables = [jnp.asarray(t) for t in transform_tables(owners, rows)]
    my_taps = lax.dynamic_slice_in_dim(short_taps, me[0] * 8, 8, 1).T

    packed = call(
        pack_kernel,
        shape((owners, 24, rows), BF16),
        [ANY] * 2,
        [pltpu.VMEM((rows, width), BF16), pltpu.VMEM((rows, width), F32), pltpu.SemaphoreType.DMA((2,))],
    )(inputs, filters)
    received = lax.all_to_all(packed, "seq", 0, 0, tiled=True)

    pieces = [shifted(cotangent, "chan", d) for d in (1, 2, 3)]
    grad_packed, grad_gated = call(
        cotangent_kernel,
        (shape((width, rows), BF16), shape((width, rows), F32)),
        [SMEM] + [ANY] * 3 + [VMEM] * 3,
        [
            pltpu.VMEM((rows, width), BF16),
            pltpu.VMEM(w_out.shape, BF16),
            pltpu.VMEM((rows, width), BF16),
            pltpu.SemaphoreType.DMA((3,)),
        ],
    )(me, gate_branch, w_out, cotangent, *pieces)

    def work_space(signals):
        return [
            pltpu.VMEM((2, width, rows), F32),
            pltpu.VMEM((2 * width, 4 * rows), BF16),
            pltpu.VMEM((signals * width, 2 * rows), F32),
        ]

    def traded(values):
        return [values[0]] + [
            lax.ppermute(values[d], "seq", [(i, i ^ d) for i in range(owners)]) for d in (1, 2, 3)
        ]

    sent, spectra = call(
        forward_kernel,
        (shape((owners, 16, rows), BF16), shape((2 * width, 2 * rows), F32)),
        [VMEM] * 7,
        work_space(1),
    )(my_taps, received, grad_packed, *tables)
    back = lax.all_to_all(sent, "seq", 0, 0, tiled=True)

    cot_parts = traded(
        call(
            cot_kernel,
            (shape((16, 32, rows), BF16),) * 4,
            [SMEM] + [VMEM] * 4,
            [pltpu.VMEM((16, 4, 32, rows), BF16)],
        )(me, cotangent, *pieces)
    )

    gated = call(gate_kernel, shape((rows, width), BF16), [VMEM] * 2)(back, gate_branch)
    gated_parts = traded([gated] * 4)
    grad_parts = traded(
        call(
            backward_kernel,
            (shape((16, 24, rows), BF16),) * 4,
            [SMEM] + [VMEM] * 8,
            work_space(2) + [pltpu.VMEM((16, 4, 24, rows), F32)],
        )(me, my_taps, received, back, spectra, *tables)
    )
    last = call(weight_kernel, shape((16, 208, rows), BF16), [VMEM] * 12)(*cot_parts, *gated_parts, *grad_parts)
    groups = [list(range(k, owners, 4)) for k in range(4)]
    arrived = lax.all_to_all(last, "seq", 0, 0, axis_index_groups=groups, tiled=True)

    grad_gate, own, s1, s2, s3 = call(
        project_kernel,
        (shape((rows, width), BF16), shape((rows, width), F32)) + (shape((rows, width), BF16),) * 3,
        [SMEM] + [VMEM] * 4,
    )(me, back, gated, grad_gated, w_out)
    others = [shifted(s, "chan", d) for d, s in ((1, s1), (2, s2), (3, s3))]
    output = (own + others[0].astype(F32) + others[1].astype(F32) + others[2].astype(F32)).astype(BF16)

    grad_inputs, grad_filters, grad_taps, grad_wout = call(
        unpack_kernel,
        (
            shape((rows, width), BF16),
            shape((rows, width), F32),
            shape((4, width), F32),
            shape((32, width), F32),
        ),
        [SMEM, VMEM],
        [pltpu.VMEM((3, 16, 4, 8, rows), F32)],
    )(me, arrived)
    return (output, grad_inputs, grad_gate, grad_filters, grad_taps, grad_wout.T)


def solution(mesh):
    in_specs = (
        P("seq", "chan"),
        P("seq", "chan"),
        P(None, "chan"),
        P("seq", "chan"),
        P("chan", None),
        P("seq", "chan"),
    )
    out_specs = (
        P("seq", "chan"),
        P("seq", "chan"),
        P("seq", "chan"),
        P("seq", "chan"),
        P(None, "chan"),
        P("chan", "seq"),
    )
    return jax.shard_map(local, mesh=mesh, in_specs=in_specs, out_specs=out_specs, check_vma=False)
```

```python
import functools
import math

import jax
import jax.numpy as jnp
import ml_dtypes
import numpy as np
from jax import lax
from jax.experimental import pallas as pl
from jax.experimental.pallas import tpu as pltpu
from jax.sharding import PartitionSpec as P

F32 = jnp.float32
BF16 = jnp.bfloat16
VMEM = pl.BlockSpec(memory_space=pltpu.VMEM)
SMEM = pl.BlockSpec(memory_space=pltpu.SMEM)
HBM = pl.BlockSpec(memory_space=pltpu.HBM)


def split_table(table):
    high = table.astype(ml_dtypes.bfloat16)
    low = (table - high.astype(np.float64)).astype(ml_dtypes.bfloat16)
    return high, low


def transform_tables(coarse, fine):
    length = coarse * fine
    k1 = np.arange(coarse)[:, None] + 0.25
    angle = 2.0 * math.pi * k1 * np.arange(coarse)[None, :] / coarse
    first = np.concatenate([np.cos(angle), -np.sin(angle)], 0)
    last = np.concatenate([np.cos(angle).T, -np.sin(angle).T], 1)
    angle = 2.0 * math.pi * k1 * np.arange(fine)[None, :] / length
    twist = np.concatenate([np.cos(angle), np.sin(angle)], 0)
    angle = 2.0 * math.pi * (np.outer(np.arange(fine), np.arange(fine)) % fine) / fine
    cos, sin = np.cos(angle), np.sin(angle)
    forward = np.concatenate([np.concatenate([cos, -sin], 1), np.concatenate([sin, cos], 1)], 0)
    inverse = np.concatenate([np.concatenate([cos, sin], 1), np.concatenate([-sin, cos], 1)], 0) / length
    high, low = split_table(first)
    pad = np.zeros((2 * coarse, 2 * fine - 3 * coarse), high.dtype)
    rows = [*split_table(forward), *split_table(inverse), np.concatenate([high, high, low, pad], 1)]
    high, low = split_table(last)
    rows.append(np.concatenate([high, high], 1))
    rows.append(np.concatenate([low, np.zeros_like(low)], 1))
    rows.append(np.concatenate(split_table(twist), 1))
    return np.concatenate(rows, 0)


class Tables:
    def __init__(self, ref, coarse, fine):
        size = 2 * fine
        self.ref, self.size, self.coarse, self.fine = ref, size, coarse, fine

    def second(self, which):
        return self.ref[which * self.size : (which + 1) * self.size, :]

    def first(self):
        start = 4 * self.size
        return self.ref[start : start + 2 * self.coarse, : 3 * self.coarse]

    def last(self):
        start = 4 * self.size + 2 * self.coarse
        return jnp.concatenate(
            [
                self.ref[start : start + self.coarse, :],
                self.ref[start + self.coarse : start + 2 * self.coarse, : 2 * self.coarse],
            ],
            1,
        )

    def twist(self):
        start = 4 * self.size + 4 * self.coarse
        both = self.ref[start : start + 2 * self.coarse, :].astype(F32)
        both = both[:, : self.fine] + both[:, self.fine :]
        return both[: self.coarse], both[self.coarse :]


def split(value):
    high = value.astype(BF16)
    return high, (value - high.astype(F32)).astype(BF16)


def dot(a, b, dims=(((1,), (0,)), ((), ()))):
    return lax.dot_general(a, b, dims, preferred_element_type=F32)


NT = (((1,), (1,)), ((), ()))


def load(sources, buffers, sems):
    copies = [pltpu.make_async_copy(src, dst, sems.at[i]) for i, (src, dst) in enumerate(zip(sources, buffers))]
    for copy in copies:
        copy.start()
    for copy in copies:
        copy.wait()


def far(value):
    return pltpu.with_memory_space_constraint(value, pltpu.HBM)


def pack_kernel(inputs_hbm, filters_hbm, out_ref, inputs_ref, filters_ref, sems):
    load((inputs_hbm, filters_hbm), (inputs_ref, filters_ref), sems)
    owners = out_ref.shape[0]
    filters = filters_ref[...].T
    high = filters.astype(BF16).astype(F32)
    rows = [inputs_ref[...].astype(F32).T, high, filters - high]
    rows = [r.reshape(owners, 8, r.shape[1]) for r in rows]
    out_ref[...] = jnp.concatenate(rows, 1).astype(BF16)


def own_kernel(me_ref, gate_hbm, piece_hbm, w_ref, part_ref, gate_out, gate_ref, piece, sems):
    load((gate_hbm, piece_hbm), (gate_ref, piece), sems)
    width = gate_ref.shape[1]
    cols = pl.ds(pl.multiple_of(me_ref[1] * width, width), width)
    part_ref[...] = dot(w_ref[:, cols], piece[...], NT)
    gate_out[...] = gate_ref[...].astype(F32).T


def cotangent_kernel(me_ref, gate_ref, part_ref, w_ref, c1, c2, c3, out_ref, gg_ref):
    chan = me_ref[1]
    width = gate_ref.shape[0]
    total = part_ref[...]
    for step, piece in enumerate((c1, c2, c3)):
        owner = lax.rem(chan + 3 - step, 4)
        cols = pl.ds(pl.multiple_of(owner * width, width), width)
        total = total + dot(w_ref[:, cols], piece[...], NT)
    gg_ref[...] = total
    out_ref[...] = (total * gate_ref[...]).astype(BF16)


def cot_kernel(me_ref, c0, c1, c2, c3, o0, o1, o2, o3, scratch):
    kind = lax.rem(me_ref[0], 4)
    chan = me_ref[1]
    for step, piece in enumerate((c0, c1, c2, c3)):
        owner = lax.rem(chan + 4 - step, 4)
        flipped = piece[...].astype(F32).T.astype(BF16)
        scratch[pl.ds(owner * 4, 4)] = flipped.reshape(4, 4, 32, flipped.shape[1])
    for d, out in enumerate((o0, o1, o2, o3)):
        out[...] = scratch[:, kind ^ d]


def delayed(value, t):
    if t == 0:
        return value
    lane = lax.broadcasted_iota(jnp.int32, value.shape, 2)
    turned = pltpu.roll(value, t, 2)
    before = jnp.concatenate([jnp.zeros_like(turned[:1]), turned[:-1]], 0)
    return jnp.where(lane < t, before, turned)


def coarse_stage(sig, s, tables, stage):
    blocks, fine = tables.coarse, tables.fine
    twist_re, twist_im = tables.twist()
    first = tables.first()
    for pair in range(4):
        both = jnp.concatenate([sig[s, pl.ds(2 * pair + h, blocks, stride=8), :] for h in range(2)], 1)
        high, low = split(both)
        coarse = dot(first, jnp.concatenate([high, low, high], 0))
        for h in range(2):
            re = coarse[:blocks, h * fine : (h + 1) * fine]
            im = coarse[blocks:, h * fine : (h + 1) * fine]
            put(stage, s, 2 * pair + h, re * twist_re + im * twist_im, im * twist_re - re * twist_im)


def put(stage, s, c, re, im):
    blocks, fine = re.shape
    rows = pl.ds((s * 8 + c) * blocks, blocks)
    high, low = split(jnp.concatenate([re, im], 1))
    stage[rows, : 2 * fine] = high
    stage[rows, 2 * fine :] = low


def fine_stage(stage, s, tables, which):
    count = stage.shape[1]
    rows = pl.ds(s * count, count)
    high = stage[rows, : stage.shape[1] // 2]
    low = stage[rows, stage.shape[1] // 2 :]
    table = tables.second(which)
    return dot(high, table) + dot(low, table) + dot(high, tables.second(which + 1))


def back_stage(spec, s, tables, sig):
    blocks, fine = tables.coarse, tables.fine
    twist_re, twist_im = tables.twist()
    last = tables.last()
    for pair in range(4):
        halves = []
        for h in range(2):
            rows = pl.ds((s * 8 + 2 * pair + h) * blocks, blocks)
            re, im = spec[rows, :fine], spec[rows, fine:]
            halves.append(jnp.concatenate([re * twist_re - im * twist_im, im * twist_re + re * twist_im], 0))
        high, low = split(jnp.concatenate(halves, 1))
        back = dot(last, jnp.concatenate([high, low, high], 0))
        for h in range(2):
            sig[s, pl.ds(2 * pair + h, blocks, stride=8), :] = back[:, h * fine : (h + 1) * fine]


def forward_kernel(taps_ref, recv_ref, grad_ref, table_ref, out_ref, spec, sig, stage, work):
    blocks, _, fine = recv_ref.shape
    count = 8 * blocks
    tables = Tables(table_ref, blocks, fine)
    taps = taps_ref[...]
    received = recv_ref[...].astype(F32)
    given = received[:, 0:8]
    mixed = jnp.zeros_like(given)
    for t in range(4):
        mixed = mixed + taps[:, t : t + 1][None] * delayed(given, t)
    sig[0] = mixed.reshape(count, fine)
    sig[1] = (received[:, 8:16] + received[:, 16:24]).reshape(count, fine)
    for s in range(2):
        coarse_stage(sig, s, tables, stage)
    for s in range(2):
        spec[pl.ds(s * count, count), :] = fine_stage(stage, s, tables, 0)
    for c in range(8):
        (mr, mi), (fr, fi) = (
            (spec[pl.ds((s * 8 + c) * blocks, blocks), :fine], spec[pl.ds((s * 8 + c) * blocks, blocks), fine:])
            for s in range(2)
        )
        put(stage, 0, c, mr * fr - mi * fi, mr * fi + mi * fr)
    work[...] = fine_stage(stage, 0, tables, 2)
    back_stage(work, 0, tables, sig)
    convolved = sig[0].reshape(blocks, 8, fine)
    grad_conv = grad_ref[...].astype(F32).reshape(blocks, 8, fine)
    out_ref[...] = jnp.concatenate([convolved, grad_conv], 1).astype(BF16)


def backward_kernel(
    me_ref, _, taps_ref, recv_ref, back_ref, spec, table_ref,
    o0, o1, o2, o3, sig, stage, work, parts
):
    blocks, _, fine = recv_ref.shape
    count = 8 * blocks
    tables = Tables(table_ref, blocks, fine)
    taps = taps_ref[...]
    sig[0] = back_ref[...].astype(F32)[:, 8:16].reshape(count, fine)
    coarse_stage(sig, 0, tables, stage)
    work[pl.ds(0, count), :] = fine_stage(stage, 0, tables, 0)
    for c in range(8):
        rows = pl.ds(c * blocks, blocks)
        gr, gi = work[rows, :fine], work[rows, fine:]
        for s in range(2):
            rows = pl.ds(((1 - s) * 8 + c) * blocks, blocks)
            re, im = spec[rows, :fine], spec[rows, fine:]
            put(stage, s, c, re * gr + im * gi, re * gi - im * gr)
    for s in range(2):
        work[pl.ds(s * count, count), :] = fine_stage(stage, s, tables, 2)
    for s in range(2):
        back_stage(work, s, tables, sig)
    grad_mixed, grad_filters = (sig[s].reshape(blocks, 8, fine) for s in range(2))
    lane = lax.broadcasted_iota(jnp.int32, (blocks, 8, fine), 2)
    zero = jnp.zeros((1, 8, fine), F32)
    grad_inputs = taps[:, 0:1][None] * grad_mixed
    for t in range(1, 4):
        turned = pltpu.roll(grad_mixed, fine - t, 2)
        ahead = jnp.where(lane >= fine - t, jnp.concatenate([turned[1:], zero], 0), turned)
        grad_inputs = grad_inputs + taps[:, t : t + 1][None] * ahead
    given = recv_ref[...].astype(F32)[:, 0:8]
    column = lax.broadcasted_iota(jnp.int32, (8, fine), 1)
    tap_tile = jnp.zeros((8, fine), F32)
    for t in range(4):
        total = jnp.sum(jnp.sum(delayed(given, t) * grad_mixed, axis=0), axis=1, keepdims=True)
        high = total.astype(BF16).astype(F32)
        tap_tile = jnp.where(column == t, high, tap_tile)
        tap_tile = jnp.where(column == t + 4, total - high, tap_tile)
    parts[...] = jnp.concatenate([grad_inputs, grad_filters], 1).reshape(blocks // 4, 4, 16, fine)
    tap_tile = jnp.concatenate([tap_tile, jnp.zeros_like(tap_tile)], 0).astype(BF16)
    kind = lax.rem(me_ref[0], 4)
    for d, out in enumerate((o0, o1, o2, o3)):
        out[0 : blocks // 4] = parts[:, kind ^ d].astype(BF16)
        out[blocks // 4] = tap_tile


def gate_kernel(recv_ref, gate_ref, gated_ref):
    blocks, _, rows = recv_ref.shape
    convolved = recv_ref[...].astype(F32)[:, 0:8].reshape(blocks * 8, rows)
    gated_ref[...] = (gate_ref[...].astype(F32) * convolved.T).astype(BF16)


def weight_kernel(k0, k1, k2, k3, g0, g1, g2, g3, p0, p1, p2, p3, out_ref):
    groups, rows, depth = k0.shape
    left = jnp.concatenate([k[...].reshape(groups * rows, depth) for k in (k0, k1, k2, k3)], 1)
    total = dot(left, jnp.concatenate([g[...] for g in (g0, g1, g2, g3)], 0))
    for j in range(4):
        columns = total[:, j * depth : (j + 1) * depth].reshape(groups, rows, depth)
        out_ref[:, 64 + j * rows : 64 + (j + 1) * rows, :] = columns.astype(BF16)
    tap_rows = None
    for d, part in enumerate((p0, p1, p2, p3)):
        out_ref[:, 16 * d : 16 * (d + 1), :] = part[0:groups]
        tile = part[groups].astype(F32)
        tile = pltpu.roll(tile, 8 * d, 1) if d else tile
        tap_rows = tile if tap_rows is None else tap_rows + tile
    out_ref[:, 192:208, :] = jnp.broadcast_to(tap_rows[None], (groups, 16, depth)).astype(BF16)


def project_kernel(me_ref, recv_ref, gated_ref, gg_ref, w_ref, gate_grad_ref, own_ref, s1, s2, s3):
    chan = me_ref[1]
    blocks, _, rows = recv_ref.shape
    width = gated_ref.shape[1]
    convolved = recv_ref[...].astype(F32)[:, 0:8].reshape(width, rows)
    gate_grad_ref[...] = (gg_ref[...] * convolved).T.astype(BF16)
    for step, out in enumerate((own_ref, s1, s2, s3)):
        owner = lax.rem(chan + step, 4)
        cols = pl.ds(pl.multiple_of(owner * width, width), width)
        out[...] = dot(gated_ref[...], w_ref[:, cols]).astype(out.dtype)


def unpack_kernel(me_ref, recv_ref, gi_ref, gf_ref, taps_ref, weight_ref, scratch):
    kind = lax.rem(me_ref[0], 4)
    groups, _, rows = recv_ref.shape
    width = groups * 32
    tap_rows = recv_ref[:, 192:208, :].astype(F32)[:, 0:8]
    for d in range(4):
        value = recv_ref[:, 16 * d : 16 * (d + 1), :].astype(F32)
        source = kind ^ d
        scratch[0, :, source] = value[:, 0:8]
        scratch[1, :, source] = value[:, 8:16]
        scratch[2, :, source] = pltpu.roll(tap_rows, rows - 8 * d, 2) if d else tap_rows
    gi_ref[...] = scratch[0].reshape(width, rows).T.astype(BF16)
    gf_ref[...] = scratch[1].reshape(width, rows).T
    flat = scratch[2].reshape(width, rows).T
    taps_ref[...] = flat[0:4] + flat[4:8]
    total = jnp.sum(recv_ref[:, 64:192, :].astype(F32), axis=0)
    for j in range(4):
        weight_ref[:, j * rows : (j + 1) * rows] = total[32 * j : 32 * (j + 1)]


def call(kernel, outs, in_specs, scratch=()):
    return pl.pallas_call(
        kernel,
        out_shape=outs,
        in_specs=in_specs,
        out_specs=jax.tree.map(lambda _: VMEM, outs),
        scratch_shapes=list(scratch),
        compiler_params=pltpu.CompilerParams(vmem_limit_bytes=12 * 1024 * 1024),
    )


def shifted(value, axis, steps):
    count = lax.axis_size(axis)
    return lax.ppermute(value, axis, [(i, (i + steps) % count) for i in range(count)])


def local(inputs, gate_branch, short_taps, filters, w_out, cotangent):
    shape = jax.ShapeDtypeStruct
    owners = lax.axis_size("seq")
    rows, width = inputs.shape
    me = jnp.stack([lax.axis_index("seq"), lax.axis_index("chan")]).astype(jnp.int32)
    table = jnp.asarray(transform_tables(owners, rows))
    my_taps = lax.dynamic_slice_in_dim(short_taps, me[0] * 8, 8, 1).T

    packed = call(
        pack_kernel,
        shape((owners, 24, rows), BF16),
        [HBM] * 2,
        [pltpu.VMEM((rows, width), BF16), pltpu.VMEM((rows, width), F32), pltpu.SemaphoreType.DMA((2,))],
    )(far(inputs), far(filters))
    received = lax.all_to_all(packed, "seq", 0, 0, tiled=True)

    pieces = [shifted(cotangent, "chan", d) for d in (1, 2, 3)]
    own_part, gate_flipped = call(
        own_kernel,
        (shape((width, rows), F32),) * 2,
        [SMEM, HBM, HBM, VMEM],
        [pltpu.VMEM((rows, width), BF16)] * 2 + [pltpu.SemaphoreType.DMA((2,))],
    )(me, far(gate_branch), far(cotangent), w_out)
    grad_packed, grad_gated = call(
        cotangent_kernel,
        (shape((width, rows), BF16), shape((width, rows), F32)),
        [SMEM] + [VMEM] * 6,
    )(me, gate_flipped, own_part, w_out, *pieces)

    def work_space(signals):
        return [
            pltpu.VMEM((2, width, rows), F32),
            pltpu.VMEM((2 * width, 4 * rows), BF16),
            pltpu.VMEM((signals * width, 2 * rows), F32),
        ]

    def swapped(value, distance):
        return lax.ppermute(value, "seq", [(i, i ^ distance) for i in range(owners)])

    def traded(values):
        return [values[0]] + [swapped(values[d], d) for d in (1, 2, 3)]

    sent, spectra = call(
        forward_kernel,
        (shape((owners, 16, rows), BF16), shape((2 * width, 2 * rows), F32)),
        [VMEM] * 4,
        work_space(1),
    )(my_taps, received, grad_packed, table)
    back = lax.all_to_all(sent, "seq", 0, 0, tiled=True)

    cot_parts = traded(
        call(
            cot_kernel,
            (shape((16, 32, rows), BF16),) * 4,
            [SMEM] + [VMEM] * 4,
            [pltpu.VMEM((16, 4, 32, rows), BF16)],
        )(me, cotangent, *pieces)
    )

    gated = call(gate_kernel, shape((rows, width), BF16), [VMEM] * 2)(back, gate_branch)
    across = swapped(gated, 2)
    beside = swapped(gated, 1)
    gated_parts = [gated, beside, across, swapped(across, 1)]
    grad_parts = traded(
        call(
            backward_kernel,
            (shape((17, 16, rows), BF16),) * 4,
            [SMEM] + [VMEM] * 6,
            work_space(2) + [pltpu.VMEM((16, 4, 16, rows), F32)],
        )(me, beside, my_taps, received, back, spectra, table)
    )
    last = call(weight_kernel, shape((16, 208, rows), BF16), [VMEM] * 12)(*cot_parts, *gated_parts, *grad_parts)
    groups = [list(range(k, owners, 4)) for k in range(4)]
    arrived = lax.all_to_all(last, "seq", 0, 0, axis_index_groups=groups, tiled=True)

    grad_gate, own, s1, s2, s3 = call(
        project_kernel,
        (shape((rows, width), BF16), shape((rows, width), F32)) + (shape((rows, width), BF16),) * 3,
        [SMEM] + [VMEM] * 4,
    )(me, back, gated, grad_gated, w_out)
    others = [shifted(s, "chan", d) for d, s in ((1, s1), (2, s2), (3, s3))]
    output = (own + others[0].astype(F32) + others[1].astype(F32) + others[2].astype(F32)).astype(BF16)

    grad_inputs, grad_filters, grad_taps, grad_wout = call(
        unpack_kernel,
        (
            shape((rows, width), BF16),
            shape((rows, width), F32),
            shape((4, width), F32),
            shape((32, width), F32),
        ),
        [SMEM, VMEM],
        [pltpu.VMEM((3, 16, 4, 8, rows), F32)],
    )(me, arrived)
    return (output, grad_inputs, grad_gate, grad_filters, grad_taps, grad_wout.T)


def solution(mesh):
    in_specs = (
        P("seq", "chan"),
        P("seq", "chan"),
        P(None, "chan"),
        P("seq", "chan"),
        P("chan", None),
        P("seq", "chan"),
    )
    out_specs = (
        P("seq", "chan"),
        P("seq", "chan"),
        P("seq", "chan"),
        P("seq", "chan"),
        P(None, "chan"),
        P("chan", "seq"),
    )
    return jax.shard_map(local, mesh=mesh, in_specs=in_specs, out_specs=out_specs, check_vma=False)
```

```python
import functools
import math

import jax
import jax.numpy as jnp
import ml_dtypes
import numpy as np
from jax import lax
from jax.experimental import pallas as pl
from jax.experimental.pallas import tpu as pltpu
from jax.sharding import PartitionSpec as P

F32 = jnp.float32
BF16 = jnp.bfloat16
VMEM = pl.BlockSpec(memory_space=pltpu.VMEM)
SMEM = pl.BlockSpec(memory_space=pltpu.SMEM)
HBM = pl.BlockSpec(memory_space=pltpu.HBM)


def split_table(table):
    high = table.astype(ml_dtypes.bfloat16)
    low = (table - high.astype(np.float64)).astype(ml_dtypes.bfloat16)
    return high, low


def transform_tables(coarse, fine):
    length = coarse * fine
    k1 = np.arange(coarse)[:, None] + 0.25
    angle = 2.0 * math.pi * k1 * np.arange(coarse)[None, :] / coarse
    first = np.concatenate([np.cos(angle), -np.sin(angle)], 0)
    last = np.concatenate([np.cos(angle).T, -np.sin(angle).T], 1)
    angle = 2.0 * math.pi * k1 * np.arange(fine)[None, :] / length
    twist = np.concatenate([np.cos(angle), np.sin(angle)], 0)
    angle = 2.0 * math.pi * (np.outer(np.arange(fine), np.arange(fine)) % fine) / fine
    cos, sin = np.cos(angle), np.sin(angle)
    forward = np.concatenate([np.concatenate([cos, -sin], 1), np.concatenate([sin, cos], 1)], 0)
    inverse = np.concatenate([np.concatenate([cos, sin], 1), np.concatenate([-sin, cos], 1)], 0) / length
    high, low = split_table(first)
    pad = np.zeros((2 * coarse, 2 * fine - 3 * coarse), high.dtype)
    rows = [*split_table(forward), *split_table(inverse), np.concatenate([high, high, low, pad], 1)]
    high, low = split_table(last)
    rows.append(np.concatenate([high, high], 1))
    rows.append(np.concatenate([low, np.zeros_like(low)], 1))
    rows.append(np.concatenate(split_table(twist), 1))
    return np.concatenate(rows, 0)


class Tables:
    def __init__(self, ref, coarse, fine):
        size = 2 * fine
        self.ref, self.size, self.coarse, self.fine = ref, size, coarse, fine

    def second(self, which):
        return self.ref[which * self.size : (which + 1) * self.size, :]

    def first(self):
        start = 4 * self.size
        return self.ref[start : start + 2 * self.coarse, : 3 * self.coarse]

    def last(self):
        start = 4 * self.size + 2 * self.coarse
        return jnp.concatenate(
            [
                self.ref[start : start + self.coarse, :],
                self.ref[start + self.coarse : start + 2 * self.coarse, : 2 * self.coarse],
            ],
            1,
        )

    def twist(self):
        start = 4 * self.size + 4 * self.coarse
        both = self.ref[start : start + 2 * self.coarse, :].astype(F32)
        both = both[:, : self.fine] + both[:, self.fine :]
        return both[: self.coarse], both[self.coarse :]


def split(value):
    high = value.astype(BF16)
    return high, (value - high.astype(F32)).astype(BF16)


def dot(a, b, dims=(((1,), (0,)), ((), ()))):
    return lax.dot_general(a, b, dims, preferred_element_type=F32)


NT = (((1,), (1,)), ((), ()))


def load(sources, buffers, sems):
    copies = [pltpu.make_async_copy(src, dst, sems.at[i]) for i, (src, dst) in enumerate(zip(sources, buffers))]
    for copy in copies:
        copy.start()
    for copy in copies:
        copy.wait()


def far(value):
    return pltpu.with_memory_space_constraint(value, pltpu.HBM)


def pack_kernel(inputs_hbm, filters_hbm, out_ref, inputs_ref, filters_ref, sems):
    load((inputs_hbm, filters_hbm), (inputs_ref, filters_ref), sems)
    owners = out_ref.shape[0]
    filters = filters_ref[...].T
    high = filters.astype(BF16).astype(F32)
    rows = [inputs_ref[...].astype(F32).T, high, filters - high]
    rows = [r.reshape(owners, 8, r.shape[1]) for r in rows]
    out_ref[...] = jnp.concatenate(rows, 1).astype(BF16)


def own_kernel(me_ref, gate_hbm, piece_hbm, w_ref, part_ref, gate_out, gate_ref, piece, sems):
    load((gate_hbm, piece_hbm), (gate_ref, piece), sems)
    width = gate_ref.shape[1]
    cols = pl.ds(pl.multiple_of(me_ref[1] * width, width), width)
    part_ref[...] = dot(w_ref[:, cols], piece[...], NT)
    gate_out[...] = gate_ref[...].astype(F32).T


def cotangent_kernel(me_ref, gate_ref, part_ref, w_ref, c1, c2, c3, out_ref, gg_ref):
    chan = me_ref[1]
    width = gate_ref.shape[0]
    total = part_ref[...]
    for step, piece in enumerate((c1, c2, c3)):
        owner = lax.rem(chan + 3 - step, 4)
        cols = pl.ds(pl.multiple_of(owner * width, width), width)
        total = total + dot(w_ref[:, cols], piece[...], NT)
    gg_ref[...] = total
    out_ref[...] = (total * gate_ref[...]).astype(BF16)


def cot_kernel(me_ref, c0, c1, c2, c3, o0, o1, o2, o3, scratch):
    kind = lax.rem(me_ref[0], 4)
    chan = me_ref[1]
    for step, piece in enumerate((c0, c1, c2, c3)):
        owner = lax.rem(chan + 4 - step, 4)
        flipped = piece[...].astype(F32).T.astype(BF16)
        scratch[pl.ds(owner * 4, 4)] = flipped.reshape(4, 4, 32, flipped.shape[1])
    for d, out in enumerate((o0, o1, o2, o3)):
        out[...] = scratch[:, kind ^ d]


def delayed(value, t):
    if t == 0:
        return value
    lane = lax.broadcasted_iota(jnp.int32, value.shape, 2)
    turned = pltpu.roll(value, t, 2)
    before = jnp.concatenate([jnp.zeros_like(turned[:1]), turned[:-1]], 0)
    return jnp.where(lane < t, before, turned)


def coarse_stage(sig, s, tables, stage):
    blocks, fine = tables.coarse, tables.fine
    twist_re, twist_im = tables.twist()
    first = tables.first()
    for pair in range(4):
        both = jnp.concatenate([sig[s, pl.ds(2 * pair + h, blocks, stride=8), :] for h in range(2)], 1)
        high, low = split(both)
        coarse = dot(first, jnp.concatenate([high, low, high], 0))
        for h in range(2):
            re = coarse[:blocks, h * fine : (h + 1) * fine]
            im = coarse[blocks:, h * fine : (h + 1) * fine]
            put(stage, s, 2 * pair + h, re * twist_re + im * twist_im, im * twist_re - re * twist_im)


def put(stage, s, c, re, im):
    blocks, fine = re.shape
    rows = pl.ds((s * 8 + c) * blocks, blocks)
    high, low = split(jnp.concatenate([re, im], 1))
    stage[rows, : 2 * fine] = high
    stage[rows, 2 * fine :] = low


def fine_stage(stage, s, tables, which):
    count = stage.shape[1]
    rows = pl.ds(s * count, count)
    high = stage[rows, : stage.shape[1] // 2]
    low = stage[rows, stage.shape[1] // 2 :]
    table = tables.second(which)
    return dot(high, table) + dot(low, table) + dot(high, tables.second(which + 1))


def back_stage(spec, s, tables, sig):
    blocks, fine = tables.coarse, tables.fine
    twist_re, twist_im = tables.twist()
    last = tables.last()
    for pair in range(4):
        halves = []
        for h in range(2):
            rows = pl.ds((s * 8 + 2 * pair + h) * blocks, blocks)
            re, im = spec[rows, :fine], spec[rows, fine:]
            halves.append(jnp.concatenate([re * twist_re - im * twist_im, im * twist_re + re * twist_im], 0))
        high, low = split(jnp.concatenate(halves, 1))
        back = dot(last, jnp.concatenate([high, low, high], 0))
        for h in range(2):
            sig[s, pl.ds(2 * pair + h, blocks, stride=8), :] = back[:, h * fine : (h + 1) * fine]


def forward_kernel(taps_ref, recv_ref, grad_ref, table_ref, out_ref, spec, sig, stage, work):
    blocks, _, fine = recv_ref.shape
    count = 8 * blocks
    tables = Tables(table_ref, blocks, fine)
    taps = taps_ref[...]
    received = recv_ref[...].astype(F32)
    given = received[:, 0:8]
    mixed = jnp.zeros_like(given)
    for t in range(4):
        mixed = mixed + taps[:, t : t + 1][None] * delayed(given, t)
    sig[0] = mixed.reshape(count, fine)
    sig[1] = (received[:, 8:16] + received[:, 16:24]).reshape(count, fine)
    for s in range(2):
        coarse_stage(sig, s, tables, stage)
    for s in range(2):
        spec[pl.ds(s * count, count), :] = fine_stage(stage, s, tables, 0)
    for c in range(8):
        (mr, mi), (fr, fi) = (
            (spec[pl.ds((s * 8 + c) * blocks, blocks), :fine], spec[pl.ds((s * 8 + c) * blocks, blocks), fine:])
            for s in range(2)
        )
        put(stage, 0, c, mr * fr - mi * fi, mr * fi + mi * fr)
    work[...] = fine_stage(stage, 0, tables, 2)
    back_stage(work, 0, tables, sig)
    convolved = sig[0].reshape(blocks, 8, fine)
    grad_conv = grad_ref[...].astype(F32).reshape(blocks, 8, fine)
    out_ref[...] = jnp.concatenate([convolved, grad_conv], 1).astype(BF16)


def backward_kernel(
    me_ref, _, taps_ref, recv_ref, back_ref, spec, table_ref,
    o0, o1, o2, o3, sig, stage, work, parts
):
    blocks, _, fine = recv_ref.shape
    count = 8 * blocks
    tables = Tables(table_ref, blocks, fine)
    taps = taps_ref[...]
    sig[0] = back_ref[...].astype(F32)[:, 8:16].reshape(count, fine)
    coarse_stage(sig, 0, tables, stage)
    work[pl.ds(0, count), :] = fine_stage(stage, 0, tables, 0)
    for c in range(8):
        rows = pl.ds(c * blocks, blocks)
        gr, gi = work[rows, :fine], work[rows, fine:]
        for s in range(2):
            rows = pl.ds(((1 - s) * 8 + c) * blocks, blocks)
            re, im = spec[rows, :fine], spec[rows, fine:]
            put(stage, s, c, re * gr + im * gi, re * gi - im * gr)
    for s in range(2):
        work[pl.ds(s * count, count), :] = fine_stage(stage, s, tables, 2)
    for s in range(2):
        back_stage(work, s, tables, sig)
    grad_mixed, grad_filters = (sig[s].reshape(blocks, 8, fine) for s in range(2))
    lane = lax.broadcasted_iota(jnp.int32, (blocks, 8, fine), 2)
    zero = jnp.zeros((1, 8, fine), F32)
    grad_inputs = taps[:, 0:1][None] * grad_mixed
    for t in range(1, 4):
        turned = pltpu.roll(grad_mixed, fine - t, 2)
        ahead = jnp.where(lane >= fine - t, jnp.concatenate([turned[1:], zero], 0), turned)
        grad_inputs = grad_inputs + taps[:, t : t + 1][None] * ahead
    given = recv_ref[...].astype(F32)[:, 0:8]
    column = lax.broadcasted_iota(jnp.int32, (8, fine), 1)
    tap_tile = jnp.zeros((8, fine), F32)
    for t in range(4):
        total = jnp.sum(jnp.sum(delayed(given, t) * grad_mixed, axis=0), axis=1, keepdims=True)
        high = total.astype(BF16).astype(F32)
        tap_tile = jnp.where(column == t, high, tap_tile)
        tap_tile = jnp.where(column == t + 4, total - high, tap_tile)
    parts[...] = jnp.concatenate([grad_inputs, grad_filters], 1).reshape(blocks // 4, 4, 16, fine)
    tap_tile = jnp.concatenate([tap_tile, jnp.zeros_like(tap_tile)], 0).astype(BF16)
    kind = lax.rem(me_ref[0], 4)
    for d, out in enumerate((o0, o1, o2, o3)):
        out[0 : blocks // 4] = parts[:, kind ^ d].astype(BF16)
        out[blocks // 4] = tap_tile


def gate_kernel(recv_ref, gate_ref, gated_ref):
    blocks, _, rows = recv_ref.shape
    convolved = recv_ref[...].astype(F32)[:, 0:8].reshape(blocks * 8, rows)
    gated_ref[...] = (gate_ref[...].astype(F32) * convolved.T).astype(BF16)


def weight_kernel(k0, k1, k2, k3, g0, g1, g2, g3, p0, p1, p2, p3, out_ref):
    groups, rows, depth = k0.shape
    left = jnp.concatenate([k[...].reshape(groups * rows, depth) for k in (k0, k1, k2, k3)], 1)
    total = dot(left, jnp.concatenate([g[...] for g in (g0, g1, g2, g3)], 0))
    for j in range(4):
        columns = total[:, j * depth : (j + 1) * depth].reshape(groups, rows, depth)
        out_ref[:, 64 + j * rows : 64 + (j + 1) * rows, :] = columns.astype(BF16)
    tap_rows = None
    for d, part in enumerate((p0, p1, p2, p3)):
        out_ref[:, 16 * d : 16 * (d + 1), :] = part[0:groups]
        tile = part[groups].astype(F32)
        tile = pltpu.roll(tile, 8 * d, 1) if d else tile
        tap_rows = tile if tap_rows is None else tap_rows + tile
    out_ref[:, 192:200, :] = jnp.broadcast_to(tap_rows[None, :8], (groups, 8, depth)).astype(BF16)


def project_kernel(me_ref, recv_ref, gated_ref, gg_ref, w_ref, gate_grad_ref, own_ref, s1, s2, s3):
    chan = me_ref[1]
    blocks, _, rows = recv_ref.shape
    width = gated_ref.shape[1]
    convolved = recv_ref[...].astype(F32)[:, 0:8].reshape(width, rows)
    gate_grad_ref[...] = (gg_ref[...] * convolved).T.astype(BF16)
    for step, out in enumerate((own_ref, s1, s2, s3)):
        owner = lax.rem(chan + step, 4)
        cols = pl.ds(pl.multiple_of(owner * width, width), width)
        out[...] = dot(gated_ref[...], w_ref[:, cols]).astype(out.dtype)


def unpack_kernel(me_ref, recv_ref, gi_ref, gf_ref, taps_ref, weight_ref, scratch):
    kind = lax.rem(me_ref[0], 4)
    groups, _, rows = recv_ref.shape
    width = groups * 32
    tap_rows = recv_ref[:, 192:200, :].astype(F32)
    for d in range(4):
        value = recv_ref[:, 16 * d : 16 * (d + 1), :].astype(F32)
        source = kind ^ d
        scratch[0, :, source] = value[:, 0:8]
        scratch[1, :, source] = value[:, 8:16]
        scratch[2, :, source] = pltpu.roll(tap_rows, rows - 8 * d, 2) if d else tap_rows
    gi_ref[...] = scratch[0].reshape(width, rows).T.astype(BF16)
    gf_ref[...] = scratch[1].reshape(width, rows).T
    flat = scratch[2].reshape(width, rows).T
    taps_ref[...] = flat[0:4] + flat[4:8]
    total = jnp.sum(recv_ref[:, 64:192, :].astype(F32), axis=0)
    for j in range(4):
        weight_ref[:, j * rows : (j + 1) * rows] = total[32 * j : 32 * (j + 1)]


def call(kernel, outs, in_specs, scratch=()):
    return pl.pallas_call(
        kernel,
        out_shape=outs,
        in_specs=in_specs,
        out_specs=jax.tree.map(lambda _: VMEM, outs),
        scratch_shapes=list(scratch),
        compiler_params=pltpu.CompilerParams(vmem_limit_bytes=12 * 1024 * 1024),
    )


def shifted(value, axis, steps):
    count = lax.axis_size(axis)
    return lax.ppermute(value, axis, [(i, (i + steps) % count) for i in range(count)])


def local(inputs, gate_branch, short_taps, filters, w_out, cotangent):
    shape = jax.ShapeDtypeStruct
    owners = lax.axis_size("seq")
    rows, width = inputs.shape
    me = jnp.stack([lax.axis_index("seq"), lax.axis_index("chan")]).astype(jnp.int32)
    table = jnp.asarray(transform_tables(owners, rows))
    my_taps = lax.dynamic_slice_in_dim(short_taps, me[0] * 8, 8, 1).T

    packed = call(
        pack_kernel,
        shape((owners, 24, rows), BF16),
        [HBM] * 2,
        [pltpu.VMEM((rows, width), BF16), pltpu.VMEM((rows, width), F32), pltpu.SemaphoreType.DMA((2,))],
    )(far(inputs), far(filters))
    received = lax.all_to_all(packed, "seq", 0, 0, tiled=True)

    pieces = [shifted(cotangent, "chan", d) for d in (1, 2, 3)]
    own_part, gate_flipped = call(
        own_kernel,
        (shape((width, rows), F32),) * 2,
        [SMEM, HBM, HBM, VMEM],
        [pltpu.VMEM((rows, width), BF16)] * 2 + [pltpu.SemaphoreType.DMA((2,))],
    )(me, far(gate_branch), far(cotangent), w_out)
    grad_packed, grad_gated = call(
        cotangent_kernel,
        (shape((width, rows), BF16), shape((width, rows), F32)),
        [SMEM] + [VMEM] * 6,
    )(me, gate_flipped, own_part, w_out, *pieces)

    def work_space(signals):
        return [
            pltpu.VMEM((2, width, rows), F32),
            pltpu.VMEM((2 * width, 4 * rows), BF16),
            pltpu.VMEM((signals * width, 2 * rows), F32),
        ]

    def swapped(value, distance):
        return lax.ppermute(value, "seq", [(i, i ^ distance) for i in range(owners)])

    def traded(values):
        return [values[0]] + [swapped(values[d], d) for d in (1, 2, 3)]

    sent, spectra = call(
        forward_kernel,
        (shape((owners, 16, rows), BF16), shape((2 * width, 2 * rows), F32)),
        [VMEM] * 4,
        work_space(1),
    )(my_taps, received, grad_packed, table)
    back = lax.all_to_all(sent, "seq", 0, 0, tiled=True)

    cot_parts = traded(
        call(
            cot_kernel,
            (shape((16, 32, rows), BF16),) * 4,
            [SMEM] + [VMEM] * 4,
            [pltpu.VMEM((16, 4, 32, rows), BF16)],
        )(me, cotangent, *pieces)
    )

    gated = call(gate_kernel, shape((rows, width), BF16), [VMEM] * 2)(back, gate_branch)
    across = swapped(gated, 2)
    beside = swapped(gated, 1)
    grad_pieces = call(
            backward_kernel,
            (shape((17, 16, rows), BF16),) * 4,
            [SMEM] + [VMEM] * 6,
            work_space(2) + [pltpu.VMEM((16, 4, 16, rows), F32)],
        )(me, beside, my_taps, received, back, spectra, table)
    grad_parts = traded(grad_pieces)
    across, _ = lax.optimization_barrier((across, grad_pieces[1]))
    gated_parts = [gated, beside, across, swapped(across, 1)]
    last = call(weight_kernel, shape((16, 200, rows), BF16), [VMEM] * 12)(*cot_parts, *gated_parts, *grad_parts)
    groups = [list(range(k, owners, 4)) for k in range(4)]
    arrived = lax.all_to_all(last, "seq", 0, 0, axis_index_groups=groups, tiled=True)

    grad_gate, own, s1, s2, s3 = call(
        project_kernel,
        (shape((rows, width), BF16),) + (shape((rows, width), F32),) * 4,
        [SMEM] + [VMEM] * 4,
    )(me, back, gated, grad_gated, w_out)
    others = [shifted(s, "chan", d) for d, s in ((1, s1), (2, s2), (3, s3))]
    output = (own + others[0] + others[1] + others[2]).astype(BF16)

    grad_inputs, grad_filters, grad_taps, grad_wout = call(
        unpack_kernel,
        (
            shape((rows, width), BF16),
            shape((rows, width), F32),
            shape((4, width), F32),
            shape((32, width), F32),
        ),
        [SMEM, VMEM],
        [pltpu.VMEM((3, 16, 4, 8, rows), F32)],
    )(me, arrived)
    return (output, grad_inputs, grad_gate, grad_filters, grad_taps, grad_wout.T)


def solution(mesh):
    in_specs = (
        P("seq", "chan"),
        P("seq", "chan"),
        P(None, "chan"),
        P("seq", "chan"),
        P("chan", None),
        P("seq", "chan"),
    )
    out_specs = (
        P("seq", "chan"),
        P("seq", "chan"),
        P("seq", "chan"),
        P("seq", "chan"),
        P(None, "chan"),
        P("chan", "seq"),
    )
    return jax.shard_map(local, mesh=mesh, in_specs=in_specs, out_specs=out_specs, check_vma=False)
```

```python
import functools
import math

import jax
import jax.numpy as jnp
import ml_dtypes
import numpy as np
from jax import lax
from jax.experimental import pallas as pl
from jax.experimental.pallas import tpu as pltpu
from jax.sharding import PartitionSpec as P

F32 = jnp.float32
BF16 = jnp.bfloat16
VMEM = pl.BlockSpec(memory_space=pltpu.VMEM)
SMEM = pl.BlockSpec(memory_space=pltpu.SMEM)
HBM = pl.BlockSpec(memory_space=pltpu.HBM)


def split_table(table):
    high = table.astype(ml_dtypes.bfloat16)
    low = (table - high.astype(np.float64)).astype(ml_dtypes.bfloat16)
    return high, low


def transform_tables(coarse, fine):
    length = coarse * fine
    k1 = np.arange(coarse)[:, None] + 0.25
    angle = 2.0 * math.pi * k1 * np.arange(coarse)[None, :] / coarse
    first = np.concatenate([np.cos(angle), -np.sin(angle)], 0)
    last = np.concatenate([np.cos(angle).T, -np.sin(angle).T], 1)
    angle = 2.0 * math.pi * k1 * np.arange(fine)[None, :] / length
    twist = np.concatenate([np.cos(angle), np.sin(angle)], 0)
    angle = 2.0 * math.pi * (np.outer(np.arange(fine), np.arange(fine)) % fine) / fine
    cos, sin = np.cos(angle), np.sin(angle)
    forward = np.concatenate([np.concatenate([cos, -sin], 1), np.concatenate([sin, cos], 1)], 0)
    inverse = np.concatenate([np.concatenate([cos, sin], 1), np.concatenate([-sin, cos], 1)], 0) / length
    high, low = split_table(first)
    pad = np.zeros((2 * coarse, 2 * fine - 3 * coarse), high.dtype)
    rows = [*split_table(forward), *split_table(inverse), np.concatenate([high, high, low, pad], 1)]
    high, low = split_table(last)
    rows.append(np.concatenate([high, high], 1))
    rows.append(np.concatenate([low, np.zeros_like(low)], 1))
    rows.append(np.concatenate(split_table(twist), 1))
    return np.concatenate(rows, 0)


class Tables:
    def __init__(self, ref, coarse, fine):
        size = 2 * fine
        self.ref, self.size, self.coarse, self.fine = ref, size, coarse, fine

    def second(self, which):
        return self.ref[which * self.size : (which + 1) * self.size, :]

    def first(self):
        start = 4 * self.size
        return self.ref[start : start + 2 * self.coarse, : 3 * self.coarse]

    def last(self):
        start = 4 * self.size + 2 * self.coarse
        return jnp.concatenate(
            [
                self.ref[start : start + self.coarse, :],
                self.ref[start + self.coarse : start + 2 * self.coarse, : 2 * self.coarse],
            ],
            1,
        )

    def twist(self):
        start = 4 * self.size + 4 * self.coarse
        both = self.ref[start : start + 2 * self.coarse, :].astype(F32)
        both = both[:, : self.fine] + both[:, self.fine :]
        return both[: self.coarse], both[self.coarse :]


def split(value):
    high = value.astype(BF16)
    return high, (value - high.astype(F32)).astype(BF16)


def dot(a, b, dims=(((1,), (0,)), ((), ()))):
    return lax.dot_general(a, b, dims, preferred_element_type=F32)


NT = (((1,), (1,)), ((), ()))


def load(sources, buffers, sems):
    copies = [pltpu.make_async_copy(src, dst, sems.at[i]) for i, (src, dst) in enumerate(zip(sources, buffers))]
    for copy in copies:
        copy.start()
    for copy in copies:
        copy.wait()


def far(value):
    return pltpu.with_memory_space_constraint(value, pltpu.HBM)


def pack_kernel(inputs_hbm, filters_hbm, out_ref, inputs_ref, filters_ref, sems):
    load((inputs_hbm, filters_hbm), (inputs_ref, filters_ref), sems)
    owners = out_ref.shape[0]
    filters = filters_ref[...].T
    high = filters.astype(BF16).astype(F32)
    rows = [inputs_ref[...].astype(F32).T, high, filters - high]
    rows = [r.reshape(owners, 8, r.shape[1]) for r in rows]
    out_ref[...] = jnp.concatenate(rows, 1).astype(BF16)


def own_kernel(me_ref, gate_hbm, piece_hbm, w_ref, part_ref, gate_out, gate_ref, piece, sems):
    load((gate_hbm, piece_hbm), (gate_ref, piece), sems)
    width = gate_ref.shape[1]
    cols = pl.ds(pl.multiple_of(me_ref[1] * width, width), width)
    part_ref[...] = dot(w_ref[:, cols], piece[...], NT)
    gate_out[...] = gate_ref[...].astype(F32).T


def cotangent_kernel(me_ref, gate_ref, part_ref, w_ref, c1, c2, c3, out_ref):
    chan = me_ref[1]
    width = gate_ref.shape[0]
    total = part_ref[...]
    for step, piece in enumerate((c1, c2, c3)):
        owner = lax.rem(chan + 3 - step, 4)
        cols = pl.ds(pl.multiple_of(owner * width, width), width)
        total = total + dot(w_ref[:, cols], piece[...], NT)
    out_ref[...] = (total * gate_ref[...]).astype(BF16)


def cot_kernel(me_ref, c0, c1, c2, c3, o0, o1, o2, o3, scratch):
    kind = lax.rem(me_ref[0], 4)
    chan = me_ref[1]
    for step, piece in enumerate((c0, c1, c2, c3)):
        owner = lax.rem(chan + 4 - step, 4)
        flipped = piece[...].astype(F32).T.astype(BF16)
        scratch[pl.ds(owner * 4, 4)] = flipped.reshape(4, 4, 32, flipped.shape[1])
    for d, out in enumerate((o0, o1, o2, o3)):
        out[...] = scratch[:, kind ^ d]


def delayed(value, t):
    if t == 0:
        return value
    lane = lax.broadcasted_iota(jnp.int32, value.shape, 2)
    turned = pltpu.roll(value, t, 2)
    before = jnp.concatenate([jnp.zeros_like(turned[:1]), turned[:-1]], 0)
    return jnp.where(lane < t, before, turned)


def coarse_stage(sig, s, tables, stage):
    blocks, fine = tables.coarse, tables.fine
    twist_re, twist_im = tables.twist()
    first = tables.first()
    for pair in range(4):
        both = jnp.concatenate([sig[s, pl.ds(2 * pair + h, blocks, stride=8), :] for h in range(2)], 1)
        high, low = split(both)
        coarse = dot(first, jnp.concatenate([high, low, high], 0))
        for h in range(2):
            re = coarse[:blocks, h * fine : (h + 1) * fine]
            im = coarse[blocks:, h * fine : (h + 1) * fine]
            put(stage, s, 2 * pair + h, re * twist_re + im * twist_im, im * twist_re - re * twist_im)


def put(stage, s, c, re, im):
    blocks, fine = re.shape
    rows = pl.ds((s * 8 + c) * blocks, blocks)
    high, low = split(jnp.concatenate([re, im], 1))
    stage[rows, : 2 * fine] = high
    stage[rows, 2 * fine :] = low


def fine_stage(stage, s, tables, which):
    count = stage.shape[1]
    rows = pl.ds(s * count, count)
    high = stage[rows, : stage.shape[1] // 2]
    low = stage[rows, stage.shape[1] // 2 :]
    table = tables.second(which)
    return dot(high, table) + dot(low, table) + dot(high, tables.second(which + 1))


def back_stage(spec, s, tables, sig):
    blocks, fine = tables.coarse, tables.fine
    twist_re, twist_im = tables.twist()
    last = tables.last()
    for pair in range(4):
        halves = []
        for h in range(2):
            rows = pl.ds((s * 8 + 2 * pair + h) * blocks, blocks)
            re, im = spec[rows, :fine], spec[rows, fine:]
            halves.append(jnp.concatenate([re * twist_re - im * twist_im, im * twist_re + re * twist_im], 0))
        high, low = split(jnp.concatenate(halves, 1))
        back = dot(last, jnp.concatenate([high, low, high], 0))
        for h in range(2):
            sig[s, pl.ds(2 * pair + h, blocks, stride=8), :] = back[:, h * fine : (h + 1) * fine]


def forward_kernel(taps_ref, recv_ref, grad_ref, table_ref, out_ref, spec, sig, stage, work):
    blocks, _, fine = recv_ref.shape
    count = 8 * blocks
    tables = Tables(table_ref, blocks, fine)
    taps = taps_ref[...]
    received = recv_ref[...].astype(F32)
    given = received[:, 0:8]
    mixed = jnp.zeros_like(given)
    for t in range(4):
        mixed = mixed + taps[:, t : t + 1][None] * delayed(given, t)
    sig[0] = mixed.reshape(count, fine)
    sig[1] = (received[:, 8:16] + received[:, 16:24]).reshape(count, fine)
    for s in range(2):
        coarse_stage(sig, s, tables, stage)
    for s in range(2):
        spec[pl.ds(s * count, count), :] = fine_stage(stage, s, tables, 0)
    for c in range(8):
        (mr, mi), (fr, fi) = (
            (spec[pl.ds((s * 8 + c) * blocks, blocks), :fine], spec[pl.ds((s * 8 + c) * blocks, blocks), fine:])
            for s in range(2)
        )
        put(stage, 0, c, mr * fr - mi * fi, mr * fi + mi * fr)
    work[...] = fine_stage(stage, 0, tables, 2)
    back_stage(work, 0, tables, sig)
    convolved = sig[0].reshape(blocks, 8, fine)
    grad_conv = grad_ref[...].astype(F32).reshape(blocks, 8, fine)
    out_ref[...] = jnp.concatenate([convolved, grad_conv], 1).astype(BF16)


def backward_kernel(
    me_ref, _, taps_ref, recv_ref, back_ref, spec, table_ref,
    o0, o1, o2, o3, sig, stage, work, parts
):
    blocks, _, fine = recv_ref.shape
    count = 8 * blocks
    tables = Tables(table_ref, blocks, fine)
    taps = taps_ref[...]
    sig[0] = back_ref[...].astype(F32)[:, 8:16].reshape(count, fine)
    coarse_stage(sig, 0, tables, stage)
    work[pl.ds(0, count), :] = fine_stage(stage, 0, tables, 0)
    for c in range(8):
        rows = pl.ds(c * blocks, blocks)
        gr, gi = work[rows, :fine], work[rows, fine:]
        for s in range(2):
            rows = pl.ds(((1 - s) * 8 + c) * blocks, blocks)
            re, im = spec[rows, :fine], spec[rows, fine:]
            put(stage, s, c, re * gr + im * gi, re * gi - im * gr)
    for s in range(2):
        work[pl.ds(s * count, count), :] = fine_stage(stage, s, tables, 2)
    for s in range(2):
        back_stage(work, s, tables, sig)
    grad_mixed, grad_filters = (sig[s].reshape(blocks, 8, fine) for s in range(2))
    lane = lax.broadcasted_iota(jnp.int32, (blocks, 8, fine), 2)
    zero = jnp.zeros((1, 8, fine), F32)
    grad_inputs = taps[:, 0:1][None] * grad_mixed
    for t in range(1, 4):
        turned = pltpu.roll(grad_mixed, fine - t, 2)
        ahead = jnp.where(lane >= fine - t, jnp.concatenate([turned[1:], zero], 0), turned)
        grad_inputs = grad_inputs + taps[:, t : t + 1][None] * ahead
    given = recv_ref[...].astype(F32)[:, 0:8]
    column = lax.broadcasted_iota(jnp.int32, (8, fine), 1)
    tap_tile = jnp.zeros((8, fine), F32)
    for t in range(4):
        total = jnp.sum(jnp.sum(delayed(given, t) * grad_mixed, axis=0), axis=1, keepdims=True)
        high = total.astype(BF16).astype(F32)
        tap_tile = jnp.where(column == t, high, tap_tile)
        tap_tile = jnp.where(column == t + 4, total - high, tap_tile)
    parts[...] = jnp.concatenate([grad_inputs, grad_filters], 1).reshape(blocks // 4, 4, 16, fine)
    tap_tile = jnp.concatenate([tap_tile, jnp.zeros_like(tap_tile)], 0).astype(BF16)
    kind = lax.rem(me_ref[0], 4)
    for d, out in enumerate((o0, o1, o2, o3)):
        out[0 : blocks // 4] = parts[:, kind ^ d].astype(BF16)
        out[blocks // 4] = tap_tile


def gate_kernel(recv_ref, gate_ref, gated_ref):
    blocks, _, rows = recv_ref.shape
    convolved = recv_ref[...].astype(F32)[:, 0:8].reshape(blocks * 8, rows)
    gated_ref[...] = (gate_ref[...].astype(F32) * convolved.T).astype(BF16)


def weight_kernel(k0, k1, k2, k3, g0, g1, g2, g3, p0, p1, p2, p3, out_ref):
    groups, rows, depth = k0.shape
    left = jnp.concatenate([k[...].reshape(groups * rows, depth) for k in (k0, k1, k2, k3)], 1)
    total = dot(left, jnp.concatenate([g[...] for g in (g0, g1, g2, g3)], 0))
    for j in range(4):
        columns = total[:, j * depth : (j + 1) * depth].reshape(groups, rows, depth)
        out_ref[:, 64 + j * rows : 64 + (j + 1) * rows, :] = columns.astype(BF16)
    tap_rows = None
    for d, part in enumerate((p0, p1, p2, p3)):
        out_ref[:, 16 * d : 16 * (d + 1), :] = part[0:groups]
        tile = part[groups].astype(F32)
        tile = pltpu.roll(tile, 8 * d, 1) if d else tile
        tap_rows = tile if tap_rows is None else tap_rows + tile
    out_ref[:, 192:200, :] = jnp.broadcast_to(tap_rows[None, :8], (groups, 8, depth)).astype(BF16)


def gate_grad_kernel(me_ref, recv_ref, w_ref, c0, c1, c2, c3, gate_grad_ref):
    chan = me_ref[1]
    blocks, _, rows = recv_ref.shape
    width = c0.shape[1]
    total = None
    for step, piece in enumerate((c0, c1, c2, c3)):
        owner = lax.rem(chan + 4 - step, 4)
        cols = pl.ds(pl.multiple_of(owner * width, width), width)
        term = dot(w_ref[:, cols], piece[...], NT)
        total = term if total is None else total + term
    convolved = recv_ref[...].astype(F32)[:, 0:8].reshape(width, rows)
    gate_grad_ref[...] = (total * convolved).T.astype(BF16)


def project_kernel(me_ref, gated_ref, w_ref, own_ref, s1, s2, s3):
    chan = me_ref[1]
    width = gated_ref.shape[1]
    for step, out in enumerate((own_ref, s1, s2, s3)):
        owner = lax.rem(chan + step, 4)
        cols = pl.ds(pl.multiple_of(owner * width, width), width)
        out[...] = dot(gated_ref[...], w_ref[:, cols]).astype(out.dtype)


def unpack_kernel(me_ref, recv_ref, gi_ref, gf_ref, taps_ref, weight_ref, scratch):
    kind = lax.rem(me_ref[0], 4)
    groups, _, rows = recv_ref.shape
    width = groups * 32
    tap_rows = recv_ref[:, 192:200, :].astype(F32)
    for d in range(4):
        value = recv_ref[:, 16 * d : 16 * (d + 1), :].astype(F32)
        source = kind ^ d
        scratch[0, :, source] = value[:, 0:8]
        scratch[1, :, source] = value[:, 8:16]
        scratch[2, :, source] = pltpu.roll(tap_rows, rows - 8 * d, 2) if d else tap_rows
    gi_ref[...] = scratch[0].reshape(width, rows).T.astype(BF16)
    gf_ref[...] = scratch[1].reshape(width, rows).T
    flat = scratch[2].reshape(width, rows).T
    taps_ref[...] = flat[0:4] + flat[4:8]
    total = jnp.sum(recv_ref[:, 64:192, :].astype(F32), axis=0)
    for j in range(4):
        weight_ref[:, j * rows : (j + 1) * rows] = total[32 * j : 32 * (j + 1)]


def call(kernel, outs, in_specs, scratch=()):
    return pl.pallas_call(
        kernel,
        out_shape=outs,
        in_specs=in_specs,
        out_specs=jax.tree.map(lambda _: VMEM, outs),
        scratch_shapes=list(scratch),
        compiler_params=pltpu.CompilerParams(vmem_limit_bytes=12 * 1024 * 1024),
    )


def shifted(value, axis, steps):
    count = lax.axis_size(axis)
    return lax.ppermute(value, axis, [(i, (i + steps) % count) for i in range(count)])


def local(inputs, gate_branch, short_taps, filters, w_out, cotangent):
    shape = jax.ShapeDtypeStruct
    owners = lax.axis_size("seq")
    rows, width = inputs.shape
    me = jnp.stack([lax.axis_index("seq"), lax.axis_index("chan")]).astype(jnp.int32)
    table = jnp.asarray(transform_tables(owners, rows))
    my_taps = lax.dynamic_slice_in_dim(short_taps, me[0] * 8, 8, 1).T

    packed = call(
        pack_kernel,
        shape((owners, 24, rows), BF16),
        [HBM] * 2,
        [pltpu.VMEM((rows, width), BF16), pltpu.VMEM((rows, width), F32), pltpu.SemaphoreType.DMA((2,))],
    )(far(inputs), far(filters))
    received = lax.all_to_all(packed, "seq", 0, 0, tiled=True)

    pieces = [shifted(cotangent, "chan", d) for d in (1, 2, 3)]
    own_part, gate_flipped = call(
        own_kernel,
        (shape((width, rows), F32),) * 2,
        [SMEM, HBM, HBM, VMEM],
        [pltpu.VMEM((rows, width), BF16)] * 2 + [pltpu.SemaphoreType.DMA((2,))],
    )(me, far(gate_branch), far(cotangent), w_out)
    grad_packed = call(
        cotangent_kernel,
        shape((width, rows), BF16),
        [SMEM] + [VMEM] * 6,
    )(me, gate_flipped, own_part, w_out, *pieces)

    def work_space(signals):
        return [
            pltpu.VMEM((2, width, rows), F32),
            pltpu.VMEM((2 * width, 4 * rows), BF16),
            pltpu.VMEM((signals * width, 2 * rows), F32),
        ]

    def swapped(value, distance):
        return lax.ppermute(value, "seq", [(i, i ^ distance) for i in range(owners)])

    def traded(values):
        return [values[0]] + [swapped(values[d], d) for d in (1, 2, 3)]

    sent, spectra = call(
        forward_kernel,
        (shape((owners, 16, rows), BF16), shape((2 * width, 2 * rows), F32)),
        [VMEM] * 4,
        work_space(1),
    )(my_taps, received, grad_packed, table)
    back = lax.all_to_all(sent, "seq", 0, 0, tiled=True)

    cot_parts = traded(
        call(
            cot_kernel,
            (shape((16, 32, rows), BF16),) * 4,
            [SMEM] + [VMEM] * 4,
            [pltpu.VMEM((16, 4, 32, rows), BF16)],
        )(me, cotangent, *pieces)
    )

    gated = call(gate_kernel, shape((rows, width), BF16), [VMEM] * 2)(back, gate_branch)
    across = swapped(gated, 2)
    beside = swapped(gated, 1)
    grad_pieces = call(
            backward_kernel,
            (shape((17, 16, rows), BF16),) * 4,
            [SMEM] + [VMEM] * 6,
            work_space(2) + [pltpu.VMEM((16, 4, 16, rows), F32)],
        )(me, beside, my_taps, received, back, spectra, table)
    grad_parts = traded(grad_pieces)
    across, _ = lax.optimization_barrier((across, grad_pieces[1]))
    gated_parts = [gated, beside, across, swapped(across, 1)]
    grad_gate = call(gate_grad_kernel, shape((rows, width), BF16), [SMEM] + [VMEM] * 6)(
        me, back, w_out, cotangent, *pieces
    )
    last = call(weight_kernel, shape((16, 200, rows), BF16), [VMEM] * 12)(*cot_parts, *gated_parts, *grad_parts)
    groups = [list(range(k, owners, 4)) for k in range(4)]
    arrived = lax.all_to_all(last, "seq", 0, 0, axis_index_groups=groups, tiled=True)

    own, s1, s2, s3 = call(
        project_kernel, (shape((rows, width), F32),) * 4, [SMEM] + [VMEM] * 2
    )(me, gated, w_out)
    others = [shifted(s, "chan", d) for d, s in ((1, s1), (2, s2), (3, s3))]
    output = (own + others[0] + others[1] + others[2]).astype(BF16)

    grad_inputs, grad_filters, grad_taps, grad_wout = call(
        unpack_kernel,
        (
            shape((rows, width), BF16),
            shape((rows, width), F32),
            shape((4, width), F32),
            shape((32, width), F32),
        ),
        [SMEM, VMEM],
        [pltpu.VMEM((3, 16, 4, 8, rows), F32)],
    )(me, arrived)
    return (output, grad_inputs, grad_gate, grad_filters, grad_taps, grad_wout.T)


def solution(mesh):
    in_specs = (
        P("seq", "chan"),
        P("seq", "chan"),
        P(None, "chan"),
        P("seq", "chan"),
        P("chan", None),
        P("seq", "chan"),
    )
    out_specs = (
        P("seq", "chan"),
        P("seq", "chan"),
        P("seq", "chan"),
        P("seq", "chan"),
        P(None, "chan"),
        P("chan", "seq"),
    )
    return jax.shard_map(local, mesh=mesh, in_specs=in_specs, out_specs=out_specs, check_vma=False)
```
